32 devices in a mesh: groups: 2 (over y), brick: 16 (over z, x, core).
Axes of the slice: x: 2, y: 2, z: 4, core: 2. Of those that a mesh axis runs over, the one named last changes fastest.
Arguments:
- ct_win: bfloat16 [64, 128, 768], P(('groups', 'brick')), parts along dimension 0, may hold values from -8 to 8
- pet_win: bfloat16 [64, 128, 768], P(('groups', 'brick')), parts along dimension 0, may hold values from -8 to 8
- placed_anchor: int32 [64], P('groups'), parts along dimension 0, may hold values from 0 to 12, as said below
- placed_count: int32 [64], P('groups'), parts along dimension 0, may hold values from 0 to 256, as said below
- norm_ct: float32 [768], replicated, may hold values from 0.1 to 1.9
- norm_pet: float32 [768], replicated, may hold values from 0.1 to 1.9
- norm_ffn: float32 [768], replicated, may hold values from 0.1 to 1.9
- w_query: bfloat16 [768, 768], replicated, may hold values from -2 to 2
- w_key: bfloat16 [768, 768], replicated, may hold values from -2 to 2
- w_value: bfloat16 [768, 768], replicated, may hold values from -0.21875 to 0.21875
- w_out: bfloat16 [768, 768], replicated, may hold values from -0.21875 to 0.21875
- w_up: bfloat16 [768, 1536], replicated, may hold values from -0.21875 to 0.21875
- w_down: bfloat16 [1536, 768], replicated, may hold values from -0.15625 to 0.15625
- w_upconv: bfloat16 [768, 1024], replicated, may hold values from -0.21875 to 0.21875
- w_conv: bfloat16 [3456, 128], replicated, may hold values from -0.109375 to 0.109375
Outputs:
- volume: bfloat16 [64, 8, 16, 128], P(('groups', 'brick')), parts along dimension 0
The draws below stay inside these ranges and needn't reach their ends.
There are 2 independent parts, one for each index of `groups`. The reference program is written for one: setup_inputs(seed, part) draws one part's arguments, and reference() takes and returns one part's arrays. A program takes and returns all parts, laid end to end along the dimension named above; an argument that names none is the same for every part. Nothing has to cross between parts.
Inputs may be any that keep to these rules, and one draw needn't show every extreme that they name: `placed_anchor`: windows may lie anywhere in depth, whichever device holds them. `placed_count`: on each device the live slots (count above 0) are its first slots, at least one; in every draw some device has all 2 slots live and some device only one; a live window's count is 1 to 256, and 256 occurs in every draw.
All inputs are finite; a program needn't handle non-finite values.
Results may differ from the reference program's by a relative error of at most 0.012.
The reference program's roundings to bfloat16 on the way count: a program that leaves them out, or rounds other values in their place, can miss the bound.
Values may be sent and summed in bfloat16 or wider, within the bound.
No kernel may reach another device: no remote copies, remote signals or barrier semaphores. Data moves between devices by JAX's collectives and lax.ppermute only.
A program may use at most 128 MiB of HBM per device.

```python
import jax
import jax.numpy as jnp
from jax import lax

D = 768
FF = 1536
DH = 64
HEADS = 12
CH = 128
PY = 4
PX = 8
WDEP = 4
CAP = 2
PLANE = 32
WT = 128
NZ = 16
NS = 32
N_BRICK = 16


def token_pair(key):
    base = jax.random.fold_in(key, 11)
    key_one, key_two = jax.random.split(base, 2)
    shape = (NS, WT, D)
    ct_vals = jax.random.normal(key_one, shape, jnp.float32)
    pet_vals = jax.random.normal(key_two, shape, jnp.float32)
    return (jnp.clip(ct_vals, -8.0, 8.0), jnp.clip(pet_vals, -8.0, 8.0))


def draw_ct_win(key, part):
    return token_pair(key)[0].astype(jnp.bfloat16)


def draw_pet_win(key, part):
    return token_pair(key)[1].astype(jnp.bfloat16)


def projection_pair(key):
    base = jax.random.fold_in(key, 23)
    key_one, key_two = jax.random.split(base, 2)
    scale_in = D ** (-0.5)
    own_query = jax.random.normal(key_one, (D, D), jnp.float32) * scale_in
    own_key = jax.random.normal(key_two, (D, D), jnp.float32) * scale_in
    query_mat = own_query
    key_mat = own_key
    return (jnp.clip(query_mat, -2.0, 2.0), jnp.clip(key_mat, -2.0, 2.0))


def draw_w_query(key, part):
    return projection_pair(key)[0].astype(jnp.bfloat16)


def draw_w_key(key, part):
    return projection_pair(key)[1].astype(jnp.bfloat16)


def draw_placed_anchor(key, part):
    base = jax.random.fold_in(key, 53)
    key_one, key_two = jax.random.split(base, 2)
    holder = jnp.arange(NS, dtype=jnp.int32) // CAP
    slot_ids = jnp.arange(NS, dtype=jnp.int32) % CAP
    far_plane = (holder + NZ // 2) % NZ
    back = jax.random.randint(key_one, (NS,), 0, WDEP)
    far_anchor = jnp.clip(far_plane - back, 0, NZ - WDEP)
    anywhere = jax.random.randint(key_two, (NS,), 0, NZ - WDEP + 1)
    return jnp.where(slot_ids == 0, far_anchor, anywhere).astype(jnp.int32)


def draw_placed_count(key, part):
    base = jax.random.fold_in(key, 37)
    key_one, key_two, key_three = jax.random.split(base, 3)
    live_slots = jax.random.randint(key_one, (NZ,), 1, CAP + 1)
    fullest = jax.random.randint(key_two, (), 0, NZ)
    live_slots = live_slots.at[fullest].set(CAP)
    live_slots = live_slots.at[(fullest + 1) % NZ].set(1)
    slot_ids = jnp.arange(CAP, dtype=jnp.int32)[None, :]
    live_mask = slot_ids < live_slots[:, None]
    counts = jax.random.randint(key_three, (NZ, CAP), 1, 2 * WT + 1)
    counts = counts.at[fullest, 0].set(2 * WT)
    return jnp.where(live_mask, counts, 0).reshape(NZ * CAP).astype(jnp.int32)


def normal_values(key, shape, deviation, limit, kind=jnp.bfloat16):
    values = deviation * jax.random.normal(key, shape, jnp.float32)
    return jnp.clip(values, min=-limit, max=limit).astype(kind)


def setup_inputs(seed: int = 0, part: int = 0) -> dict:
    splits = jax.random.split(jax.random.key(seed), 16)
    own_keys = jax.random.split(jax.random.fold_in(splits[15], part), 16)
    ct_win = draw_ct_win(jax.random.fold_in(jax.random.fold_in(splits[15], part), 71), part)
    pet_win = draw_pet_win(jax.random.fold_in(jax.random.fold_in(splits[15], part), 71), part)
    placed_anchor = draw_placed_anchor(jax.random.fold_in(jax.random.fold_in(splits[15], part), 71), part)
    placed_count = draw_placed_count(jax.random.fold_in(jax.random.fold_in(splits[15], part), 71), part)
    norm_ct = jnp.clip(1.0 + 0.18 * jax.random.normal(splits[4], (D,), jnp.float32), 0.1, 1.9)
    norm_pet = jnp.clip(1.0 + 0.18 * jax.random.normal(splits[5], (D,), jnp.float32), 0.1, 1.9)
    norm_ffn = jnp.clip(1.0 + 0.18 * jax.random.normal(splits[6], (D,), jnp.float32), 0.1, 1.9)
    w_query = draw_w_query(jax.random.fold_in(splits[15], 71), part)
    w_key = draw_w_key(jax.random.fold_in(splits[15], 71), part)
    w_value = normal_values(splits[9], (D, D), D ** -0.5, 0.21875)
    w_out = normal_values(splits[10], (D, D), D ** -0.5, 0.21875)
    w_up = normal_values(splits[11], (D, FF), D ** -0.5, 0.21875)
    w_down = normal_values(splits[12], (FF, D), FF ** -0.5, 0.15625)
    w_upconv = normal_values(splits[13], (D, 8 * CH), D ** -0.5, 0.21875)
    w_conv = normal_values(splits[14], (27 * CH, CH), (27 * CH) ** -0.5, 0.109375)
    return dict(ct_win=ct_win, pet_win=pet_win, placed_anchor=placed_anchor, placed_count=placed_count, norm_ct=norm_ct, norm_pet=norm_pet, norm_ffn=norm_ffn, w_query=w_query, w_key=w_key, w_value=w_value, w_out=w_out, w_up=w_up, w_down=w_down, w_upconv=w_upconv, w_conv=w_conv)


epsilon = 1e-06

def rms_scale(inputs, gain_vec):
    inputs = inputs.astype(jnp.float32)
    mean_square = lax.optimization_barrier(jnp.mean(inputs * inputs, axis=-1, keepdims=True))
    return (inputs * lax.rsqrt(mean_square + epsilon) * gain_vec).astype(jnp.bfloat16)

def project(normed, weight):
    return jnp.dot(normed, weight, preferred_element_type=jnp.float32).astype(jnp.bfloat16)

def attend(queries, key_rows, value_rows):
    row_total = queries.shape[0]
    query_heads = queries.astype(jnp.float32).reshape(row_total, HEADS, DH)
    key_heads = key_rows.astype(jnp.float32).reshape(row_total, HEADS, DH)
    value_heads = value_rows.astype(jnp.float32).reshape(row_total, HEADS, DH)
    scores = jnp.einsum('whd,vhd->hwv', query_heads, key_heads) / DH ** 0.5
    row_max = lax.optimization_barrier(jnp.max(scores, axis=-1, keepdims=True))
    exp_scores = jnp.exp(scores - row_max)
    attn_probs = (exp_scores / lax.optimization_barrier(jnp.sum(exp_scores, axis=-1, keepdims=True))).astype(jnp.bfloat16)
    mixed_out = jnp.einsum('hwv,vhd->whd', attn_probs.astype(jnp.float32), value_heads)
    return mixed_out.reshape(row_total, D).astype(jnp.bfloat16)

def feed_forward(middle, norm_ffn, w_up, w_down):
    normed = rms_scale(middle, norm_ffn)
    hidden = jax.nn.gelu(jnp.dot(normed, w_up, preferred_element_type=jnp.float32), approximate=True).astype(jnp.bfloat16)
    return middle + jnp.dot(hidden, w_down, preferred_element_type=jnp.float32)

def window_layer(ct_rows, pet_rows, params):
    norm_ct, norm_pet, norm_ffn, w_query, w_key, w_value, w_out, w_up, w_down = params
    normed_ct = rms_scale(ct_rows, norm_ct)
    normed_pet = rms_scale(pet_rows, norm_pet)
    mixed_ct = attend(project(normed_ct, w_query), project(normed_pet, w_key), project(normed_pet, w_value))
    mixed_pet = attend(project(normed_pet, w_query), project(normed_ct, w_key), project(normed_ct, w_value))
    mid_ct = ct_rows.astype(jnp.float32) + jnp.dot(mixed_ct, w_out, preferred_element_type=jnp.float32)
    mid_pet = pet_rows.astype(jnp.float32) + jnp.dot(mixed_pet, w_out, preferred_element_type=jnp.float32)
    return feed_forward(mid_ct, norm_ffn, w_up, w_down) + feed_forward(mid_pet, norm_ffn, w_up, w_down)

def reference(ct_win, pet_win, placed_anchor, placed_count, norm_ct, norm_pet, norm_ffn, w_query, w_key, w_value, w_out, w_up, w_down, w_upconv, w_conv):
    params = (norm_ct, norm_pet, norm_ffn, w_query, w_key, w_value, w_out, w_up, w_down)
    offsets = jnp.arange(WDEP, dtype=jnp.float32) - (WDEP - 1) / 2.0
    spread_width = WDEP / 4.0
    bell_curve = jnp.exp(-offsets * offsets / (2.0 * spread_width * spread_width))

    def holder_step(running, holder):
        start = holder * CAP
        ct_rows = lax.dynamic_slice_in_dim(ct_win, start, CAP)
        pet_rows = lax.dynamic_slice_in_dim(pet_win, start, CAP)
        count_rows = lax.dynamic_slice_in_dim(placed_count, start, CAP)
        anchor_rows = lax.dynamic_slice_in_dim(placed_anchor, start, CAP)

        def one_slot(slot_items):
            ct_one, pet_one, count_one = slot_items
            return lax.cond(count_one > 0, lambda: window_layer(ct_one, pet_one, params), lambda: jnp.zeros((WT, D), jnp.float32))
        joined = lax.map(one_slot, (ct_rows, pet_rows, count_rows))
        factor = count_rows.astype(jnp.float32) / (2.0 * WT)
        flat_terms = (joined.reshape(CAP, WDEP, PLANE * D) * (factor[:, None] * bell_curve[None, :])[:, :, None]).reshape(CAP * WDEP, PLANE * D)
        target = (anchor_rows[:, None] + jnp.arange(WDEP, dtype=jnp.int32)[None, :]).reshape(CAP * WDEP)
        one_hot = (jnp.arange(NZ, dtype=jnp.int32)[:, None] == target[None, :]).astype(jnp.float32)
        share = jnp.dot(one_hot, flat_terms, precision=lax.Precision.HIGHEST, preferred_element_type=jnp.float32).astype(jnp.bfloat16)
        return (running + lax.optimization_barrier(share).astype(jnp.float32), None)
    numerator, unused = lax.scan(holder_step, jnp.zeros((NZ, PLANE * D), jnp.float32), jnp.arange(N_BRICK, dtype=jnp.int32))
    planes = jnp.arange(NZ, dtype=jnp.int32)
    inside = (planes[:, None] >= placed_anchor[None, :]) & (planes[:, None] < placed_anchor[None, :] + WDEP)
    shifted = (planes[:, None] - placed_anchor[None, :]).astype(jnp.float32) - (WDEP - 1) / 2.0
    all_factor = placed_count.astype(jnp.float32) / (2.0 * WT)
    denominator = lax.optimization_barrier(jnp.sum(jnp.where(inside, all_factor[None, :] * jnp.exp(-shifted * shifted / (2.0 * spread_width * spread_width)), 0.0), axis=1))
    feature = (numerator / jnp.maximum(denominator, 1.0)[:, None]).astype(jnp.bfloat16)
    up_rows = jnp.dot(feature.reshape(NZ * PLANE, D), w_upconv, preferred_element_type=jnp.float32)
    up_rows = up_rows.reshape(NZ, PY, PX, 2, 2, 2, CH).transpose(0, 3, 1, 4, 2, 5, 6)
    upsampled = up_rows.reshape(2 * NZ, 2 * PY, 2 * PX, CH).astype(jnp.bfloat16)
    active = jnp.maximum(upsampled, 0).astype(jnp.float32)
    kernel = w_conv.astype(jnp.float32).reshape(3, 3, 3, CH, CH)
    conv_out = lax.conv_general_dilated(active[None], kernel, (1, 1, 1), 'SAME', dimension_numbers=('NDHWC', 'DHWIO', 'NDHWC'), precision=lax.Precision.HIGHEST)[0]
    return (upsampled.astype(jnp.float32) + conv_out).astype(jnp.bfloat16)
```

```python
import functools
import math

import jax
import jax.numpy as jnp
from jax import lax
from jax.experimental import pallas as pl
from jax.experimental.pallas import tpu as pltpu
from jax.sharding import PartitionSpec as P

DH = 64
PY = 4
PX = 8
WDEP = 4
LANES = 128

epsilon = 1e-06

VMEM = pl.BlockSpec(memory_space=pltpu.VMEM)
SMEM = pl.BlockSpec(memory_space=pltpu.SMEM)
ANY = pl.BlockSpec(memory_space=pl.ANY)

BELL = [
    math.exp(-((i - (WDEP - 1) / 2.0) ** 2) / (2.0 * (WDEP / 4.0) ** 2)) for i in range(WDEP)
]


def rms_scale(inputs, gain_vec):
    mean_square = jnp.mean(inputs * inputs, axis=-1, keepdims=True)
    return (inputs * lax.rsqrt(mean_square + epsilon) * gain_vec).astype(jnp.bfloat16)


def dot(left, right):
    return jnp.dot(left, right, preferred_element_type=jnp.float32)


def bell_at(depth):
    value = jnp.float32(BELL[0])
    for i in range(1, WDEP):
        value = jnp.where(depth == i, jnp.float32(BELL[i]), value)
    return value


def window_kernel(
    anchor_ref,
    count_ref,
    place_ref,
    gain_ct,
    gain_pet,
    gain_ffn,
    ct_hbm,
    pet_hbm,
    wq_hbm,
    wk_hbm,
    wv_hbm,
    wo_hbm,
    wu_hbm,
    wd_hbm,
    *rest,
):
    outs = rest[:WDEP]
    tok, wq, wk, wv, wo, wu, wd, normed, q_all, k_all, v_all, mixed, sems = rest[WDEP:]
    slots, tokens, width = ct_hbm.shape
    rows = slots * tokens
    cells = tokens // WDEP
    sources = [
        (ct_hbm, tok.at[0]),
        (pet_hbm, tok.at[1]),
        (wq_hbm, wq),
        (wk_hbm, wk),
        (wv_hbm, wv),
        (wo_hbm, wo),
        (wu_hbm, wu),
        (wd_hbm, wd),
    ]
    copies = [pltpu.make_async_copy(src, dst, sems.at[i]) for i, (src, dst) in enumerate(sources)]
    for copy in copies:
        copy.start()
    position = place_ref[0]
    residue = lax.rem(position, WDEP)

    gains = (gain_ct, gain_pet)
    for m in range(2):
        copies[m].wait()
        for s in range(slots):
            start = m * rows + s * tokens
            normed[start : start + tokens, :] = rms_scale(
                tok[m, s].astype(jnp.float32), gains[m][...]
            )
    for i, (weight, result) in enumerate(((wq, q_all), (wk, k_all), (wv, v_all))):
        copies[2 + i].wait()
        result[...] = dot(normed[...], weight[...]).astype(jnp.bfloat16)

    low = lax.broadcasted_iota(jnp.int32, (tokens, LANES), 1) < DH
    zero = jnp.zeros((tokens, LANES), jnp.bfloat16)
    one = jnp.ones((tokens, LANES), jnp.bfloat16)
    ones_two = jnp.concatenate([jnp.where(low, one, zero), jnp.where(low, zero, one)], axis=0)
    for s in range(slots):
        for m in range(2):
            mine = m * rows + s * tokens
            other = (1 - m) * rows + s * tokens
            for pair in range(width // LANES):
                lanes = slice(pair * LANES, (pair + 1) * LANES)
                queries = q_all[mine : mine + tokens, lanes]
                keys = k_all[other : other + tokens, lanes]
                values = v_all[other : other + tokens, lanes]
                keys_two = jnp.concatenate(
                    [jnp.where(low, keys, zero), jnp.where(low, zero, keys)], axis=0
                )
                values_two = jnp.concatenate(
                    [jnp.where(low, values, zero), jnp.where(low, zero, values)], axis=0
                )
                scores = lax.dot_general(
                    queries,
                    keys_two,
                    (((1,), (1,)), ((), ())),
                    preferred_element_type=jnp.float32,
                )
                powers = []
                for h in range(2):
                    part = scores[:, h * tokens : (h + 1) * tokens]
                    top = jnp.max(part, axis=-1, keepdims=True)
                    powers.append(jnp.exp((part - top) * (1.0 / DH**0.5)).astype(jnp.bfloat16))
                powers = jnp.concatenate(powers, axis=1)
                both = dot(powers, jnp.concatenate([values_two, ones_two], axis=1))
                mixed[mine : mine + tokens, lanes] = (both[:, :LANES] / both[:, LANES:]).astype(
                    jnp.bfloat16
                )

    copies[5].wait()
    for phase in range(2):
        rels = (2, 3) if phase == 0 else (1, 0)
        picks = []
        for rel in rels:
            for s in range(slots):
                slot = lax.div(position, 1) * slots + s
                depth = lax.rem((residue ^ rel) + WDEP * NWRAP - anchor_ref[slot], WDEP)
                picks.append((rel, s, slot, depth))
        base = []
        picked = []
        for m in range(2):
            for rel, s, slot, depth in picks:
                offset = pl.multiple_of(depth * cells, cells)
                base.append(tok[m, s, pl.ds(offset, cells), :])
                place = pl.multiple_of(m * rows + s * tokens + depth * cells, cells)
                picked.append(mixed[pl.ds(place, cells), :])
        mid = jnp.concatenate(base, axis=0).astype(jnp.float32) + dot(
            jnp.concatenate(picked, axis=0), wo[...]
        )
        normed_mid = rms_scale(mid, gain_ffn[...])
        if phase == 0:
            copies[6].wait()
        hidden = jax.nn.gelu(dot(normed_mid, wu[...]), approximate=True)
        half = hidden.shape[0] // 2
        hidden_sum = (hidden[:half] + hidden[half:]).astype(jnp.bfloat16)
        if phase == 0:
            copies[7].wait()
        joined = mid[:half] + mid[half:] + dot(hidden_sum, wd[...])
        for j, (rel, s, slot, depth) in enumerate(picks):
            factor = jnp.full((1, width), count_ref[slot], jnp.int32).astype(jnp.float32) * (
                1.0 / (2.0 * tokens)
            )
            outs[rel][s] = (
                joined[j * cells : (j + 1) * cells] * (factor * bell_at(depth))
            ).astype(jnp.bfloat16)


NWRAP = 1 << 20


def window_call(position, anchor, count, gains, ct_win, pet_win, weights):
    slots, tokens, width = ct_win.shape
    rows = 2 * slots * tokens
    cells = tokens // WDEP
    out = jax.ShapeDtypeStruct((slots, cells, width), jnp.bfloat16)
    token_buffer = pltpu.VMEM((2, slots, tokens, width), jnp.bfloat16)
    big = pltpu.VMEM((rows, width), jnp.bfloat16)
    return pl.pallas_call(
        window_kernel,
        out_shape=[out] * WDEP,
        in_specs=[SMEM, SMEM, SMEM, VMEM, VMEM, VMEM] + [ANY] * 8,
        out_specs=[VMEM] * WDEP,
        scratch_shapes=[token_buffer]
        + [pltpu.VMEM(w.shape, w.dtype) for w in weights]
        + [big] * 5
        + [pltpu.SemaphoreType.DMA((8,))],
        compiler_params=pltpu.CompilerParams(vmem_limit_bytes=48 * 1024 * 1024),
        name="window_layer",
    )(anchor, count, position, *gains, ct_win, pet_win, *weights)


def gather_kernel(outer, anchor_ref, place_ref, *refs):
    sources = refs[:WDEP]
    kept, sent, total = refs[WDEP], refs[WDEP + 1 : -1], refs[-1]
    slots = sources[0].shape[0]
    position = place_ref[0]
    residue = lax.rem(position, WDEP)
    block = lax.div(position, WDEP)
    total[...] = jnp.zeros_like(total)
    for rel in range(WDEP):
        for s in range(slots):
            slot = (block * WDEP + (residue ^ rel)) * slots + s
            start = anchor_ref[slot]
            depth = lax.rem(residue + WDEP * NWRAP - start, WDEP)
            target = lax.div(start + depth, WDEP)
            step = target ^ block
            total[step] += sources[rel][s].astype(jnp.float32)
    kept[...] = total[0]
    for k in range(1, outer):
        sent[k - 1][...] = total[k].astype(jnp.bfloat16)


def gather_call(outer, position, anchor, blocks):
    slots, cells, width = blocks[0].shape
    return pl.pallas_call(
        functools.partial(gather_kernel, outer),
        out_shape=[jax.ShapeDtypeStruct((cells, width), jnp.float32)]
        + [jax.ShapeDtypeStruct((cells, width), jnp.bfloat16)] * (outer - 1),
        in_specs=[SMEM, SMEM] + [VMEM] * WDEP,
        out_specs=[VMEM] * outer,
        scratch_shapes=[pltpu.VMEM((outer, cells, width), jnp.float32)],
        name="plane_sum",
    )(anchor, position, *blocks)


def upconv_kernel(tokens, place_ref, anchor_ref, count_ref, kept, *refs):
    pieces = refs[:-5]
    weight, up_ref, first_ref, second_ref, grid = refs[-5:]
    channels = up_ref.shape[-1]
    position = place_ref[0]
    shift = position - anchor_ref[...]
    inside = (shift >= 0) & (shift < WDEP)
    centred = shift.astype(jnp.float32) - (WDEP - 1) / 2.0
    spread = WDEP / 4.0
    terms = (
        count_ref[...].astype(jnp.float32)
        / (2.0 * tokens)
        * jnp.exp(-centred * centred / (2.0 * spread * spread))
    )
    total = jnp.sum(jnp.where(inside, terms, 0.0), axis=-1, keepdims=True)
    numerator = kept[...]
    for piece in pieces:
        numerator = numerator + piece[...].astype(jnp.float32)
    feature = (numerator / jnp.maximum(total, 1.0)).astype(jnp.bfloat16)
    up_rows = dot(feature, weight[...])
    for a in range(2):
        for b in range(2):
            for c in range(2):
                chunk = (a * 2 + b) * 2 + c
                for y in range(PY):
                    grid[a, 2 * y + b, pl.ds(c, PX, stride=2), :] = up_rows[
                        y * PX : (y + 1) * PX, chunk * channels : (chunk + 1) * channels
                    ]
    upsampled = grid[...].astype(jnp.bfloat16)
    up_ref[...] = upsampled
    even = lax.rem(position, 2) == 0
    active = jnp.maximum(upsampled, jnp.zeros((), jnp.bfloat16))
    first_ref[...] = jnp.where(even, active[1], active[0])
    second_ref[...] = jnp.where(even, active[0], active[1])


def upconv_call(tokens, channels, position, anchor, count, kept, pieces, weight):
    layer = (2 * PY, 2 * PX, channels)
    return pl.pallas_call(
        functools.partial(upconv_kernel, tokens),
        out_shape=[
            jax.ShapeDtypeStruct((2,) + layer, jnp.bfloat16),
            jax.ShapeDtypeStruct(layer, jnp.bfloat16),
            jax.ShapeDtypeStruct(layer, jnp.bfloat16),
        ],
        in_specs=[SMEM] + [VMEM] * (4 + len(pieces)),
        out_specs=[VMEM] * 3,
        scratch_shapes=[pltpu.VMEM((2,) + layer, jnp.float32)],
        name="upconv",
    )(position, anchor[None, :], count[None, :], kept, *pieces, weight)


def conv_kernel(place_ref, up_ref, first_ref, second_ref, weight, out_ref, padded, patches):
    depth, height, breadth, channels = up_ref.shape
    even = lax.rem(place_ref[0], 2) == 0
    padded[...] = jnp.zeros_like(padded)
    for z in range(depth + 2):
        if z == 0:
            layer = jnp.where(even, second_ref[...], first_ref[...])
        elif z == depth + 1:
            layer = jnp.where(even, first_ref[...], second_ref[...])
        else:
            layer = jnp.maximum(up_ref[z - 1], jnp.zeros((), jnp.bfloat16))
        padded[z, 1 : height + 1, 8 : 8 + breadth, :] = layer.astype(jnp.float32)
    rows = height * breadth
    for z in range(depth + 2):
        for dx in range(3):
            column = padded[z, :, 7 + dx : 7 + dx + breadth, :].astype(jnp.bfloat16)
            for dy in range(3):
                tap = dy * 3 + dx
                patches[z * rows : (z + 1) * rows, tap * channels : (tap + 1) * channels] = column[
                    dy : dy + height
                ].reshape(rows, channels)
    span = 9 * channels
    total = up_ref[...].reshape(depth * rows, channels).astype(jnp.float32)
    for dz in range(3):
        total = total + dot(
            patches[dz * rows : (dz + depth) * rows, :], weight[dz * span : (dz + 1) * span, :]
        )
    out_ref[...] = total.astype(jnp.bfloat16).reshape(out_ref.shape)


def conv_call(position, upsampled, first, second, weight):
    depth, height, breadth, channels = upsampled.shape
    return pl.pallas_call(
        conv_kernel,
        out_shape=jax.ShapeDtypeStruct(upsampled.shape, jnp.bfloat16),
        in_specs=[SMEM, VMEM, VMEM, VMEM, VMEM],
        out_specs=VMEM,
        scratch_shapes=[
            pltpu.VMEM((depth + 2, height + 2, breadth + 16, channels), jnp.float32),
            pltpu.VMEM(((depth + 2) * height * breadth, 9 * channels), jnp.bfloat16),
        ],
        name="conv",
    )(position, upsampled, first, second, weight)


def swap(values, distance, total):
    return lax.ppermute(values, "brick", [(i, i ^ distance) for i in range(total)])


def on_device(
    ct_win,
    pet_win,
    placed_anchor,
    placed_count,
    norm_ct,
    norm_pet,
    norm_ffn,
    w_query,
    w_key,
    w_value,
    w_out,
    w_up,
    w_down,
    w_upconv,
    w_conv,
):
    tokens = ct_win.shape[1]
    channels = w_conv.shape[1]
    total = lax.axis_size("brick")
    outer = total // WDEP
    position = lax.axis_index("brick").reshape(1)
    blocks = window_call(
        position,
        placed_anchor,
        placed_count,
        (norm_ct[None, :], norm_pet[None, :], norm_ffn[None, :]),
        ct_win,
        pet_win,
        (w_query, w_key, w_value, w_out, w_up, w_down),
    )
    arrived = {rel: swap(blocks[rel], rel, total) for rel in (2, 3, 1)}
    sums = gather_call(
        outer, position, placed_anchor, [blocks[0]] + [arrived[rel] for rel in range(1, WDEP)]
    )
    pieces = [swap(sums[k], k * WDEP, total) for k in range(1, outer)]
    upsampled, first, second = upconv_call(
        tokens, channels, position, placed_anchor, placed_count, sums[0], pieces, w_upconv
    )
    pairs = [(i, i + 1) for i in range(1, total - 1, 2)]
    near = swap(first, 1, total)
    far = lax.ppermute(second, "brick", pairs + [(j, i) for i, j in pairs])
    return conv_call(position, upsampled, near, far, w_conv)


def solution(mesh):
    return jax.shard_map(
        on_device,
        mesh=mesh,
        in_specs=(
            P(("groups", "brick"), None, None),
            P(("groups", "brick"), None, None),
            P("groups"),
            P("groups"),
            P(),
            P(),
            P(),
            P(),
            P(),
            P(),
            P(),
            P(),
            P(),
            P(),
            P(),
        ),
        out_specs=P(("groups", "brick"), None, None, None),
        check_vma=False,
    )
```

```python
import functools
import math

import jax
import jax.numpy as jnp
from jax import lax
from jax.experimental import pallas as pl
from jax.experimental.pallas import tpu as pltpu
from jax.sharding import PartitionSpec as P

DH = 64
PY = 4
PX = 8
WDEP = 4
LANES = 128

epsilon = 1e-06

VMEM = pl.BlockSpec(memory_space=pltpu.VMEM)
SMEM = pl.BlockSpec(memory_space=pltpu.SMEM)
ANY = pl.BlockSpec(memory_space=pl.ANY)

BELL = [
    math.exp(-((i - (WDEP - 1) / 2.0) ** 2) / (2.0 * (WDEP / 4.0) ** 2)) for i in range(WDEP)
]


def rms_scale(inputs, gain_vec):
    mean_square = jnp.mean(inputs * inputs, axis=-1, keepdims=True)
    return (inputs * lax.rsqrt(mean_square + epsilon) * gain_vec).astype(jnp.bfloat16)


def dot(left, right):
    return jnp.dot(left, right, preferred_element_type=jnp.float32)


def bell_at(depth):
    value = jnp.float32(BELL[0])
    for i in range(1, WDEP):
        value = jnp.where(depth == i, jnp.float32(BELL[i]), value)
    return value


def window_kernel(
    anchor_ref,
    count_ref,
    place_ref,
    gain_ct_hbm,
    gain_pet_hbm,
    gain_ffn_hbm,
    ct_hbm,
    pet_hbm,
    wq_hbm,
    wk_hbm,
    wv_hbm,
    wo_hbm,
    wu_hbm,
    wd_hbm,
    *rest,
):
    outs = rest[:WDEP]
    gains = rest[WDEP : WDEP + 3]
    tok, wq, wk, wv, wo, wu, wd, normed, q_all, k_all, v_all, mixed, sems = rest[WDEP + 3 :]
    slots, tokens, width = ct_hbm.shape
    rows = slots * tokens
    cells = tokens // WDEP
    sources = [
        (ct_hbm, tok.at[0]),
        (pet_hbm, tok.at[1]),
        (wq_hbm, wq),
        (wk_hbm, wk),
        (wv_hbm, wv),
        (wo_hbm, wo),
        (wu_hbm, wu),
        (wd_hbm, wd),
        (gain_ct_hbm, gains[0]),
        (gain_pet_hbm, gains[1]),
        (gain_ffn_hbm, gains[2]),
    ]
    copies = [pltpu.make_async_copy(src, dst, sems.at[i]) for i, (src, dst) in enumerate(sources)]
    for i in (8, 9, 10, 0, 1, 2, 3, 4, 5, 6, 7):
        copies[i].start()
    position = place_ref[0]
    residue = lax.rem(position, WDEP)

    for i in (8, 9, 10):
        copies[i].wait()
    for m in range(2):
        copies[m].wait()
        for s in range(slots):
            start = m * rows + s * tokens
            normed[start : start + tokens, :] = rms_scale(
                tok[m, s].astype(jnp.float32), gains[m][...][None, :]
            )
    for i, (weight, result) in enumerate(((wq, q_all), (wk, k_all), (wv, v_all))):
        copies[2 + i].wait()
        result[...] = dot(normed[...], weight[...]).astype(jnp.bfloat16)

    low = lax.broadcasted_iota(jnp.int32, (tokens, LANES), 1) < DH
    zero = jnp.zeros((tokens, LANES), jnp.bfloat16)
    one = jnp.ones((tokens, LANES), jnp.bfloat16)
    ones_two = jnp.concatenate([jnp.where(low, one, zero), jnp.where(low, zero, one)], axis=0)
    for s in range(slots):
        for m in range(2):
            mine = m * rows + s * tokens
            other = (1 - m) * rows + s * tokens
            for pair in range(width // LANES):
                lanes = slice(pair * LANES, (pair + 1) * LANES)
                queries = q_all[mine : mine + tokens, lanes]
                keys = k_all[other : other + tokens, lanes]
                values = v_all[other : other + tokens, lanes]
                keys_two = jnp.concatenate(
                    [jnp.where(low, keys, zero), jnp.where(low, zero, keys)], axis=0
                )
                values_two = jnp.concatenate(
                    [jnp.where(low, values, zero), jnp.where(low, zero, values)], axis=0
                )
                scores = lax.dot_general(
                    queries,
                    keys_two,
                    (((1,), (1,)), ((), ())),
                    preferred_element_type=jnp.float32,
                )
                powers = []
                for h in range(2):
                    part = scores[:, h * tokens : (h + 1) * tokens]
                    top = jnp.max(part, axis=-1, keepdims=True)
                    powers.append(jnp.exp((part - top) * (1.0 / DH**0.5)).astype(jnp.bfloat16))
                powers = jnp.concatenate(powers, axis=1)
                both = dot(powers, jnp.concatenate([values_two, ones_two], axis=1))
                mixed[mine : mine + tokens, lanes] = (both[:, :LANES] / both[:, LANES:]).astype(
                    jnp.bfloat16
                )

    copies[5].wait()
    for phase in range(2):
        rels = (2, 3) if phase == 0 else (1, 0)
        picks = []
        for rel in rels:
            for s in range(slots):
                slot = lax.div(position, 1) * slots + s
                depth = lax.rem((residue ^ rel) + WDEP * NWRAP - anchor_ref[slot], WDEP)
                picks.append((rel, s, slot, depth))
        base = []
        picked = []
        for m in range(2):
            for rel, s, slot, depth in picks:
                offset = pl.multiple_of(depth * cells, cells)
                base.append(tok[m, s, pl.ds(offset, cells), :])
                place = pl.multiple_of(m * rows + s * tokens + depth * cells, cells)
                picked.append(mixed[pl.ds(place, cells), :])
        mid = jnp.concatenate(base, axis=0).astype(jnp.float32) + dot(
            jnp.concatenate(picked, axis=0), wo[...]
        )
        normed_mid = rms_scale(mid, gains[2][...][None, :])
        if phase == 0:
            copies[6].wait()
        hidden = jax.nn.gelu(dot(normed_mid, wu[...]), approximate=True)
        half = hidden.shape[0] // 2
        hidden_sum = (hidden[:half] + hidden[half:]).astype(jnp.bfloat16)
        if phase == 0:
            copies[7].wait()
        joined = mid[:half] + mid[half:] + dot(hidden_sum, wd[...])
        for j, (rel, s, slot, depth) in enumerate(picks):
            factor = jnp.full((1, width), count_ref[slot], jnp.int32).astype(jnp.float32) * (
                1.0 / (2.0 * tokens)
            )
            outs[rel][s] = (
                joined[j * cells : (j + 1) * cells] * (factor * bell_at(depth))
            ).astype(jnp.bfloat16)


NWRAP = 1 << 20


def in_hbm(array):
    return pltpu.with_memory_space_constraint(array, pltpu.HBM)


def in_vmem(array):
    return pltpu.with_memory_space_constraint(array, pltpu.VMEM)


SMALL = pltpu.CompilerParams(vmem_limit_bytes=12 * 1024 * 1024)


def window_call(position, anchor, count, gains, ct_win, pet_win, weights):
    slots, tokens, width = ct_win.shape
    rows = 2 * slots * tokens
    cells = tokens // WDEP
    out = pltpu.VMEM((slots, cells, width), jnp.bfloat16)
    token_buffer = pltpu.VMEM((2, slots, tokens, width), jnp.bfloat16)
    big = pltpu.VMEM((rows, width), jnp.bfloat16)
    return pl.pallas_call(
        window_kernel,
        out_shape=[out] * WDEP,
        in_specs=[SMEM, SMEM, SMEM] + [ANY] * 11,
        out_specs=[VMEM] * WDEP,
        scratch_shapes=[pltpu.VMEM((width,), jnp.float32)] * 3
        + [token_buffer]
        + [pltpu.VMEM(w.shape, w.dtype) for w in weights]
        + [big] * 5
        + [pltpu.SemaphoreType.DMA((11,))],
        compiler_params=pltpu.CompilerParams(vmem_limit_bytes=40 * 1024 * 1024),
        name="window_layer",
    )(in_hbm(anchor), in_hbm(count), position, *map(in_hbm, (*gains, ct_win, pet_win, *weights)))


def gather_kernel(outer, anchor_ref, place_ref, *refs):
    sources = refs[:WDEP]
    kept, sent, total = refs[WDEP], refs[WDEP + 1 : -1], refs[-1]
    slots = sources[0].shape[0]
    position = place_ref[0]
    residue = lax.rem(position, WDEP)
    block = lax.div(position, WDEP)
    total[...] = jnp.zeros_like(total)
    for rel in range(WDEP):
        for s in range(slots):
            slot = (block * WDEP + (residue ^ rel)) * slots + s
            start = anchor_ref[slot]
            depth = lax.rem(residue + WDEP * NWRAP - start, WDEP)
            target = lax.div(start + depth, WDEP)
            step = target ^ block
            total[step] += sources[rel][s].astype(jnp.float32)
    kept[...] = total[0]
    for k in range(1, outer):
        sent[k - 1][...] = total[k].astype(jnp.bfloat16)


def gather_call(outer, position, anchor, blocks):
    slots, cells, width = blocks[0].shape
    return pl.pallas_call(
        functools.partial(gather_kernel, outer),
        out_shape=[pltpu.VMEM((cells, width), jnp.float32)]
        + [pltpu.VMEM((cells, width), jnp.bfloat16)] * (outer - 1),
        in_specs=[SMEM, SMEM] + [VMEM] * WDEP,
        out_specs=[VMEM] * outer,
        scratch_shapes=[pltpu.VMEM((outer, cells, width), jnp.float32)],
        compiler_params=SMALL,
        name="plane_sum",
    )(in_hbm(anchor), position, *map(in_vmem, blocks))


def upconv_kernel(tokens, place_ref, anchor_ref, count_ref, kept, *refs):
    pieces = refs[:-5]
    weight, up_ref, first_ref, second_ref, grid = refs[-5:]
    channels = up_ref.shape[-1]
    position = place_ref[0]
    shift = position - anchor_ref[...]
    inside = (shift >= 0) & (shift < WDEP)
    centred = shift.astype(jnp.float32) - (WDEP - 1) / 2.0
    spread = WDEP / 4.0
    terms = (
        count_ref[...].astype(jnp.float32)
        / (2.0 * tokens)
        * jnp.exp(-centred * centred / (2.0 * spread * spread))
    )
    total = jnp.sum(jnp.where(inside, terms, 0.0), axis=-1, keepdims=True)
    numerator = kept[...]
    for piece in pieces:
        numerator = numerator + piece[...].astype(jnp.float32)
    feature = (numerator / jnp.maximum(total, 1.0)).astype(jnp.bfloat16)
    up_rows = dot(feature, weight[...])
    for a in range(2):
        for b in range(2):
            for c in range(2):
                chunk = (a * 2 + b) * 2 + c
                for y in range(PY):
                    grid[a, 2 * y + b, pl.ds(c, PX, stride=2), :] = up_rows[
                        y * PX : (y + 1) * PX, chunk * channels : (chunk + 1) * channels
                    ]
    upsampled = grid[...].astype(jnp.bfloat16)
    up_ref[...] = upsampled
    even = lax.rem(position, 2) == 0
    active = jnp.maximum(upsampled, jnp.zeros((), jnp.bfloat16))
    first_ref[...] = jnp.where(even, active[1], active[0])
    second_ref[...] = jnp.where(even, active[0], active[1])


def upconv_call(tokens, channels, position, anchor, count, kept, pieces, weight):
    layer = (2 * PY, 2 * PX, channels)
    return pl.pallas_call(
        functools.partial(upconv_kernel, tokens),
        out_shape=[
            pltpu.VMEM((2,) + layer, jnp.bfloat16),
            pltpu.VMEM(layer, jnp.bfloat16),
            pltpu.VMEM(layer, jnp.bfloat16),
        ],
        in_specs=[SMEM] + [VMEM] * (4 + len(pieces)),
        out_specs=[VMEM] * 3,
        scratch_shapes=[pltpu.VMEM((2,) + layer, jnp.float32)],
        compiler_params=SMALL,
        name="upconv",
    )(position, in_hbm(anchor[None, :]), in_hbm(count[None, :]), *map(in_vmem, (kept, *pieces, weight)))


def conv_kernel(place_ref, up_ref, first_ref, second_ref, weight, out_ref, padded, patches):
    depth, height, breadth, channels = up_ref.shape
    even = lax.rem(place_ref[0], 2) == 0
    padded[...] = jnp.zeros_like(padded)
    for z in range(depth + 2):
        if z == 0:
            layer = jnp.where(even, second_ref[...], first_ref[...])
        elif z == depth + 1:
            layer = jnp.where(even, first_ref[...], second_ref[...])
        else:
            layer = jnp.maximum(up_ref[z - 1], jnp.zeros((), jnp.bfloat16))
        padded[z, 1 : height + 1, 8 : 8 + breadth, :] = layer.astype(jnp.float32)
    rows = height * breadth
    for z in range(depth + 2):
        for dx in range(3):
            column = padded[z, :, 7 + dx : 7 + dx + breadth, :].astype(jnp.bfloat16)
            for dy in range(3):
                tap = dy * 3 + dx
                patches[z * rows : (z + 1) * rows, tap * channels : (tap + 1) * channels] = column[
                    dy : dy + height
                ].reshape(rows, channels)
    span = 9 * channels
    total = up_ref[...].reshape(depth * rows, channels).astype(jnp.float32)
    for dz in range(3):
        total = total + dot(
            patches[dz * rows : (dz + depth) * rows, :], weight[dz * span : (dz + 1) * span, :]
        )
    out_ref[...] = total.astype(jnp.bfloat16).reshape(out_ref.shape)


def conv_call(position, upsampled, first, second, weight):
    depth, height, breadth, channels = upsampled.shape
    return pl.pallas_call(
        conv_kernel,
        out_shape=jax.ShapeDtypeStruct(upsampled.shape, jnp.bfloat16),
        in_specs=[SMEM, VMEM, VMEM, VMEM, VMEM],
        out_specs=VMEM,
        scratch_shapes=[
            pltpu.VMEM((depth + 2, height + 2, breadth + 16, channels), jnp.float32),
            pltpu.VMEM(((depth + 2) * height * breadth, 9 * channels), jnp.bfloat16),
        ],
        compiler_params=SMALL,
        name="conv",
    )(position, *map(in_vmem, (upsampled, first, second, weight)))


def swap(values, distance, total):
    return lax.ppermute(values, "brick", [(i, i ^ distance) for i in range(total)])


def on_device(
    ct_win,
    pet_win,
    placed_anchor,
    placed_count,
    norm_ct,
    norm_pet,
    norm_ffn,
    w_query,
    w_key,
    w_value,
    w_out,
    w_up,
    w_down,
    w_upconv,
    w_conv,
):
    tokens = ct_win.shape[1]
    channels = w_conv.shape[1]
    total = lax.axis_size("brick")
    outer = total // WDEP
    position = lax.axis_index("brick").reshape(1)
    blocks = window_call(
        position,
        placed_anchor,
        placed_count,
        (norm_ct, norm_pet, norm_ffn),
        ct_win,
        pet_win,
        (w_query, w_key, w_value, w_out, w_up, w_down),
    )
    arrived = {rel: swap(blocks[rel], rel, total) for rel in (2, 3, 1)}
    sums = gather_call(
        outer, position, placed_anchor, [blocks[0]] + [arrived[rel] for rel in range(1, WDEP)]
    )
    pieces = [swap(sums[k], k * WDEP, total) for k in range(1, outer)]
    upsampled, first, second = upconv_call(
        tokens, channels, position, placed_anchor, placed_count, sums[0], pieces, w_upconv
    )
    pairs = [(i, i + 1) for i in range(1, total - 1, 2)]
    near = swap(first, 1, total)
    far = lax.ppermute(second, "brick", pairs + [(j, i) for i, j in pairs])
    return conv_call(position, upsampled, near, far, w_conv)


def solution(mesh):
    return jax.shard_map(
        on_device,
        mesh=mesh,
        in_specs=(
            P(("groups", "brick"), None, None),
            P(("groups", "brick"), None, None),
            P("groups"),
            P("groups"),
            P(),
            P(),
            P(),
            P(),
            P(),
            P(),
            P(),
            P(),
            P(),
            P(),
            P(),
        ),
        out_specs=P(("groups", "brick"), None, None, None),
        check_vma=False,
    )
```

```python
import functools
import math

import jax
import jax.numpy as jnp
from jax import lax
from jax.experimental import pallas as pl
from jax.experimental.pallas import tpu as pltpu
from jax.sharding import PartitionSpec as P

DH = 64
PY = 4
PX = 8
WDEP = 4
LANES = 128

epsilon = 1e-06

VMEM = pl.BlockSpec(memory_space=pltpu.VMEM)
SMEM = pl.BlockSpec(memory_space=pltpu.SMEM)
ANY = pl.BlockSpec(memory_space=pl.ANY)

BELL = [
    math.exp(-((i - (WDEP - 1) / 2.0) ** 2) / (2.0 * (WDEP / 4.0) ** 2)) for i in range(WDEP)
]


def rms_scale(inputs, gain_vec):
    mean_square = jnp.mean(inputs * inputs, axis=-1, keepdims=True)
    return (inputs * lax.rsqrt(mean_square + epsilon) * gain_vec).astype(jnp.bfloat16)


def dot(left, right):
    return jnp.dot(left, right, preferred_element_type=jnp.float32)


def bell_at(depth):
    value = jnp.float32(BELL[0])
    for i in range(1, WDEP):
        value = jnp.where(depth == i, jnp.float32(BELL[i]), value)
    return value


def ffn_rows(base, mixed_rows, gain_row, wo, wu, wd, before_up=None, before_down=None):
    mid = base.astype(jnp.float32) + dot(mixed_rows, wo[...])
    normed_mid = rms_scale(mid, gain_row)
    if before_up is not None:
        before_up()
    hidden = jax.nn.gelu(dot(normed_mid, wu[...]), approximate=True)
    half = hidden.shape[0] // 2
    hidden_sum = (hidden[:half] + hidden[half:]).astype(jnp.bfloat16)
    if before_down is not None:
        before_down()
    return mid[:half] + mid[half:] + dot(hidden_sum, wd[...])


def window_kernel(*refs):
    sources, outs, scratch = refs[:13], refs[13:22], refs[22:]
    gain_refs = (scratch[0], scratch[1], outs[8])
    anchor_ref, count_ref, tok, wq, wk, wv, normed, q_all, k_all, v_all, mixed, sems = scratch[2:]
    far_out = outs[:2]
    rest_mixed, rest_base, rest_scale, wo, wu, wd = outs[2:8]
    slots, tokens, width = sources[5].shape
    rows = slots * tokens
    cells = tokens // WDEP
    targets = (
        anchor_ref,
        count_ref,
        *gain_refs,
        tok.at[0],
        tok.at[1],
        wq,
        wk,
        wv,
        wo,
        wu,
        wd,
    )
    copies = [
        pltpu.make_async_copy(src, dst, sems.at[i])
        for i, (src, dst) in enumerate(zip(sources, targets, strict=True))
    ]
    for i in (2, 3, 5, 6, 7, 0, 1, 4, 8, 9, 10, 11, 12):
        copies[i].start()
    position = lax.axis_index("brick")
    residue = lax.rem(position, WDEP)

    copies[2].wait()
    copies[3].wait()
    for m in range(2):
        copies[5 + m].wait()
        for s in range(slots):
            start = m * rows + s * tokens
            normed[start : start + tokens, :] = rms_scale(
                tok[m, s].astype(jnp.float32), gain_refs[m][...][None, :]
            )
    for i, (weight, result) in enumerate(((wq, q_all), (wk, k_all), (wv, v_all))):
        copies[7 + i].wait()
        result[...] = dot(normed[...], weight[...]).astype(jnp.bfloat16)

    low = lax.broadcasted_iota(jnp.int32, (tokens, LANES), 1) < DH
    zero = jnp.zeros((tokens, LANES), jnp.bfloat16)
    one = jnp.ones((tokens, LANES), jnp.bfloat16)
    ones_two = jnp.concatenate([jnp.where(low, one, zero), jnp.where(low, zero, one)], axis=0)
    for s in range(slots):
        for m in range(2):
            mine = m * rows + s * tokens
            other = (1 - m) * rows + s * tokens
            for pair in range(width // LANES):
                lanes = slice(pair * LANES, (pair + 1) * LANES)
                queries = q_all[mine : mine + tokens, lanes]
                keys = k_all[other : other + tokens, lanes]
                values = v_all[other : other + tokens, lanes]
                keys_two = jnp.concatenate(
                    [jnp.where(low, keys, zero), jnp.where(low, zero, keys)], axis=0
                )
                values_two = jnp.concatenate(
                    [jnp.where(low, values, zero), jnp.where(low, zero, values)], axis=0
                )
                scores = lax.dot_general(
                    queries,
                    keys_two,
                    (((1,), (1,)), ((), ())),
                    preferred_element_type=jnp.float32,
                )
                powers = []
                for h in range(2):
                    part = scores[:, h * tokens : (h + 1) * tokens]
                    top = jnp.max(part, axis=-1, keepdims=True)
                    powers.append(jnp.exp((part - top) * (1.0 / DH**0.5)).astype(jnp.bfloat16))
                powers = jnp.concatenate(powers, axis=1)
                both = dot(powers, jnp.concatenate([values_two, ones_two], axis=1))
                mixed[mine : mine + tokens, lanes] = (both[:, :LANES] / both[:, LANES:]).astype(
                    jnp.bfloat16
                )

    for i in (0, 1, 4, 10):
        copies[i].wait()

    def picked(rels):
        picks, base, chosen = [], [], []
        for rel in rels:
            for s in range(slots):
                slot = position * slots + s
                depth = lax.rem((residue ^ rel) + WDEP * NWRAP - anchor_ref[slot], WDEP)
                factor = jnp.full((1, LANES), count_ref[slot], jnp.int32).astype(jnp.float32) * (
                    1.0 / (2.0 * tokens)
                )
                picks.append((s, depth, factor * bell_at(depth)))
        for m in range(2):
            for s, depth, _ in picks:
                base.append(tok[m, s, pl.ds(pl.multiple_of(depth * cells, cells), cells), :])
                place = pl.multiple_of(m * rows + s * tokens + depth * cells, cells)
                chosen.append(mixed[pl.ds(place, cells), :])
        return (
            [scale for _, _, scale in picks],
            jnp.concatenate(base, axis=0),
            jnp.concatenate(chosen, axis=0),
        )

    scales, base, chosen = picked((1, 0))
    rest_base[...] = base
    rest_mixed[...] = chosen
    for j, scale in enumerate(scales):
        rest_scale[j * cells : (j + 1) * cells, :] = jnp.broadcast_to(scale, (cells, LANES))
    scales, base, chosen = picked((2, 3))
    joined = ffn_rows(
        base, chosen, gain_refs[2][...][None, :], wo, wu, wd, copies[11].wait, copies[12].wait
    )
    for j, scale in enumerate(scales):
        far_out[j // slots][j % slots] = (
            joined[j * cells : (j + 1) * cells] * scale[:, :1]
        ).astype(jnp.bfloat16)


def near_kernel(rest_mixed, rest_base, rest_scale, wo, wu, wd, gain, near_out, own_out):
    slots, cells, width = near_out.shape
    joined = ffn_rows(rest_base[...], rest_mixed[...], gain[...][None, :], wo, wu, wd)
    joined = (joined * rest_scale[:, :1]).astype(jnp.bfloat16)
    for j, out in enumerate((near_out, own_out)):
        for s in range(slots):
            start = (j * slots + s) * cells
            out[s] = joined[start : start + cells]


NWRAP = 1 << 20
ARRIVAL = (2, 3, 1, 0)


def in_hbm(array):
    return pltpu.with_memory_space_constraint(array, pltpu.HBM)


def in_vmem(array):
    return pltpu.with_memory_space_constraint(array, pltpu.VMEM)


SMALL = pltpu.CompilerParams(vmem_limit_bytes=12 * 1024 * 1024)


def window_call(anchor, count, gains, ct_win, pet_win, weights):
    slots, tokens, width = ct_win.shape
    rows = 2 * slots * tokens
    cells = tokens // WDEP
    half = slots * (WDEP // 2) * cells
    out = pltpu.VMEM((slots, cells, width), jnp.bfloat16)
    rest = pltpu.VMEM((2 * half, width), jnp.bfloat16)
    big = pltpu.VMEM((rows, width), jnp.bfloat16)
    far_two, far_three, *passed = pl.pallas_call(
        window_kernel,
        out_shape=[out, out, rest, rest, pltpu.VMEM((half, LANES), jnp.float32)]
        + [pltpu.VMEM(w.shape, w.dtype) for w in weights[3:]]
        + [pltpu.VMEM((width,), jnp.float32)],
        in_specs=[ANY] * 13,
        out_specs=[VMEM] * 9,
        scratch_shapes=[pltpu.VMEM((width,), jnp.float32)] * 2
        + [pltpu.SMEM(anchor.shape, jnp.int32)] * 2
        + [pltpu.VMEM((2, slots, tokens, width), jnp.bfloat16)]
        + [pltpu.VMEM(w.shape, w.dtype) for w in weights[:3]]
        + [big] * 5
        + [pltpu.SemaphoreType.DMA((13,))],
        compiler_params=pltpu.CompilerParams(vmem_limit_bytes=28 * 1024 * 1024),
        name="window_layer",
    )(*map(in_hbm, (anchor, count, *gains, ct_win, pet_win, *weights)))
    near, own = pl.pallas_call(
        near_kernel,
        out_shape=[out, out],
        in_specs=[VMEM] * 7,
        out_specs=[VMEM] * 2,
        compiler_params=SMALL,
        cost_estimate=pl.CostEstimate(
            flops=2 * half * width * (2 * width + 3 * weights[4].shape[1]),
            bytes_accessed=4 * half * width,
            transcendentals=0,
        ),
        name="near_rows",
    )(*map(in_vmem, passed))
    return own, near, far_two, far_three


def gather_kernel(outer, anchor_ref, place_ref, *refs):
    sources = refs[:WDEP]
    kept, sent, total = refs[WDEP], refs[WDEP + 1 : -1], refs[-1]
    slots = sources[0].shape[0]
    position = place_ref[0]
    residue = lax.rem(position, WDEP)
    block = lax.div(position, WDEP)
    total[...] = jnp.zeros_like(total)
    for source, rel in zip(sources, ARRIVAL, strict=True):
        for s in range(slots):
            slot = (block * WDEP + (residue ^ rel)) * slots + s
            start = anchor_ref[slot]
            depth = lax.rem(residue + WDEP * NWRAP - start, WDEP)
            target = lax.div(start + depth, WDEP)
            step = target ^ block
            total[step] += source[s].astype(jnp.float32)
    kept[...] = total[0]
    for k in range(1, outer):
        sent[k - 1][...] = total[k].astype(jnp.bfloat16)


def gather_call(outer, position, anchor, blocks):
    slots, cells, width = blocks[0].shape
    return pl.pallas_call(
        functools.partial(gather_kernel, outer),
        out_shape=[pltpu.VMEM((cells, width), jnp.float32)]
        + [pltpu.VMEM((cells, width), jnp.bfloat16)] * (outer - 1),
        in_specs=[SMEM, SMEM] + [VMEM] * WDEP,
        out_specs=[VMEM] * outer,
        scratch_shapes=[pltpu.VMEM((outer, cells, width), jnp.float32)],
        compiler_params=SMALL,
        name="plane_sum",
    )(in_hbm(anchor), position, *map(in_vmem, blocks))


def upconv_kernel(tokens, place_ref, anchor_ref, count_ref, kept, *refs):
    pieces = refs[:-5]
    weight, up_ref, first_ref, second_ref, grid = refs[-5:]
    channels = up_ref.shape[-1]
    position = place_ref[0]
    shift = position - anchor_ref[...]
    inside = (shift >= 0) & (shift < WDEP)
    centred = shift.astype(jnp.float32) - (WDEP - 1) / 2.0
    spread = WDEP / 4.0
    terms = (
        count_ref[...].astype(jnp.float32)
        / (2.0 * tokens)
        * jnp.exp(-centred * centred / (2.0 * spread * spread))
    )
    total = jnp.sum(jnp.where(inside, terms, 0.0), axis=-1, keepdims=True)
    numerator = kept[...]
    for piece in pieces:
        numerator = numerator + piece[...].astype(jnp.float32)
    feature = (numerator / jnp.maximum(total, 1.0)).astype(jnp.bfloat16)
    up_rows = dot(feature, weight[...])
    for a in range(2):
        for b in range(2):
            for c in range(2):
                chunk = (a * 2 + b) * 2 + c
                for y in range(PY):
                    grid[a, 2 * y + b, pl.ds(c, PX, stride=2), :] = up_rows[
                        y * PX : (y + 1) * PX, chunk * channels : (chunk + 1) * channels
                    ]
    upsampled = grid[...].astype(jnp.bfloat16)
    up_ref[...] = upsampled
    even = lax.rem(position, 2) == 0
    active = jnp.maximum(upsampled, jnp.zeros((), jnp.bfloat16))
    first_ref[...] = jnp.where(even, active[1], active[0])
    second_ref[...] = jnp.where(even, active[0], active[1])


def upconv_call(tokens, channels, position, anchor, count, kept, pieces, weight):
    layer = (2 * PY, 2 * PX, channels)
    return pl.pallas_call(
        functools.partial(upconv_kernel, tokens),
        out_shape=[
            pltpu.VMEM((2,) + layer, jnp.bfloat16),
            pltpu.VMEM(layer, jnp.bfloat16),
            pltpu.VMEM(layer, jnp.bfloat16),
        ],
        in_specs=[SMEM] + [VMEM] * (4 + len(pieces)),
        out_specs=[VMEM] * 3,
        scratch_shapes=[pltpu.VMEM((2,) + layer, jnp.float32)],
        compiler_params=SMALL,
        name="upconv",
    )(position, in_hbm(anchor[None, :]), in_hbm(count[None, :]), *map(in_vmem, (kept, *pieces, weight)))


def conv_kernel(place_ref, up_ref, first_ref, second_ref, weight, out_ref, padded, patches):
    depth, height, breadth, channels = up_ref.shape
    even = lax.rem(place_ref[0], 2) == 0
    padded[...] = jnp.zeros_like(padded)
    for z in range(depth + 2):
        if z == 0:
            layer = jnp.where(even, second_ref[...], first_ref[...])
        elif z == depth + 1:
            layer = jnp.where(even, first_ref[...], second_ref[...])
        else:
            layer = jnp.maximum(up_ref[z - 1], jnp.zeros((), jnp.bfloat16))
        padded[z, 1 : height + 1, 8 : 8 + breadth, :] = layer.astype(jnp.float32)
    rows = height * breadth
    for z in range(depth + 2):
        for dx in range(3):
            column = padded[z, :, 7 + dx : 7 + dx + breadth, :].astype(jnp.bfloat16)
            for dy in range(3):
                tap = dy * 3 + dx
                patches[z * rows : (z + 1) * rows, tap * channels : (tap + 1) * channels] = column[
                    dy : dy + height
                ].reshape(rows, channels)
    span = 9 * channels
    total = up_ref[...].reshape(depth * rows, channels).astype(jnp.float32)
    for dz in range(3):
        total = total + dot(
            patches[dz * rows : (dz + depth) * rows, :], weight[dz * span : (dz + 1) * span, :]
        )
    out_ref[...] = total.astype(jnp.bfloat16).reshape(out_ref.shape)


def conv_call(position, upsampled, first, second, weight):
    depth, height, breadth, channels = upsampled.shape
    return pl.pallas_call(
        conv_kernel,
        out_shape=jax.ShapeDtypeStruct(upsampled.shape, jnp.bfloat16),
        in_specs=[SMEM, VMEM, VMEM, VMEM, VMEM],
        out_specs=VMEM,
        scratch_shapes=[
            pltpu.VMEM((depth + 2, height + 2, breadth + 16, channels), jnp.float32),
            pltpu.VMEM(((depth + 2) * height * breadth, 9 * channels), jnp.bfloat16),
        ],
        compiler_params=SMALL,
        name="conv",
    )(position, *map(in_vmem, (upsampled, first, second, weight)))


def swap(values, distance, total):
    return lax.ppermute(values, "brick", [(i, i ^ distance) for i in range(total)])


def on_device(
    ct_win,
    pet_win,
    placed_anchor,
    placed_count,
    norm_ct,
    norm_pet,
    norm_ffn,
    w_query,
    w_key,
    w_value,
    w_out,
    w_up,
    w_down,
    w_upconv,
    w_conv,
):
    tokens = ct_win.shape[1]
    channels = w_conv.shape[1]
    total = lax.axis_size("brick")
    outer = total // WDEP
    position = lax.axis_index("brick").reshape(1)
    blocks = window_call(
        placed_anchor,
        placed_count,
        (norm_ct, norm_pet, norm_ffn),
        ct_win,
        pet_win,
        (w_query, w_key, w_value, w_out, w_up, w_down),
    )
    own, near, far_two, far_three = blocks
    far_two, far_three = swap(far_two, 2, total), swap(far_three, 3, total)
    near, far_two = lax.optimization_barrier((near, far_two))
    arrived = (far_two, far_three, swap(near, 1, total), own)
    sums = gather_call(outer, position, placed_anchor, arrived)
    pieces = [swap(sums[k], k * WDEP, total) for k in range(outer - 1, 0, -1)]
    upsampled, first, second = upconv_call(
        tokens, channels, position, placed_anchor, placed_count, sums[0], pieces, w_upconv
    )
    pairs = [(i, i + 1) for i in range(1, total - 1, 2)]
    near = swap(first, 1, total)
    far = lax.ppermute(second, "brick", pairs + [(j, i) for i, j in pairs])
    return conv_call(position, upsampled, near, far, w_conv)


def solution(mesh):
    return jax.shard_map(
        on_device,
        mesh=mesh,
        in_specs=(
            P(("groups", "brick"), None, None),
            P(("groups", "brick"), None, None),
            P("groups"),
            P("groups"),
            P(),
            P(),
            P(),
            P(),
            P(),
            P(),
            P(),
            P(),
            P(),
            P(),
            P(),
        ),
        out_specs=P(("groups", "brick"), None, None, None),
        check_vma=False,
    )
```

```python
import functools
import math

import jax
import jax.numpy as jnp
from jax import lax
from jax.experimental import pallas as pl
from jax.experimental.pallas import tpu as pltpu
from jax.sharding import PartitionSpec as P

DH = 64
PY = 4
PX = 8
WDEP = 4
LANES = 128

epsilon = 1e-06

VMEM = pl.BlockSpec(memory_space=pltpu.VMEM)
SMEM = pl.BlockSpec(memory_space=pltpu.SMEM)
ANY = pl.BlockSpec(memory_space=pl.ANY)

BELL = [
    math.exp(-((i - (WDEP - 1) / 2.0) ** 2) / (2.0 * (WDEP / 4.0) ** 2)) for i in range(WDEP)
]


def rms_scale(inputs, gain_vec):
    mean_square = jnp.mean(inputs * inputs, axis=-1, keepdims=True)
    return (inputs * lax.rsqrt(mean_square + epsilon) * gain_vec).astype(jnp.bfloat16)


def dot(left, right):
    return jnp.dot(left, right, preferred_element_type=jnp.float32)


def bell_at(depth):
    value = jnp.float32(BELL[0])
    for i in range(1, WDEP):
        value = jnp.where(depth == i, jnp.float32(BELL[i]), value)
    return value


def ffn_rows(base, mixed, gain_row, wo, wu, wd, normed, hidden, before_up=None, before_down=None):
    half = normed.shape[0] // 2
    total = jnp.zeros((half, normed.shape[1]), jnp.float32)
    for m in range(2):
        rows = slice(m * half, (m + 1) * half)
        mid = base[rows].astype(jnp.float32) + dot(mixed[rows], wo[...])
        normed[rows, :] = rms_scale(mid, gain_row)
        total = total + mid
    if before_up is not None:
        before_up()
    chunk = hidden.shape[1] // 2
    for c in range(2):
        columns = slice(c * chunk, (c + 1) * chunk)
        both = [
            jax.nn.gelu(dot(normed[m * half : (m + 1) * half, :], wu[:, columns]), approximate=True)
            for m in range(2)
        ]
        hidden[:, columns] = (both[0] + both[1]).astype(jnp.bfloat16)
    if before_down is not None:
        before_down()
    return total + dot(hidden[...], wd[...])


def attend(query_ref, key_ref, value_ref, result, place, start, tokens):
    width = query_ref.shape[1]
    low = lax.broadcasted_iota(jnp.int32, (tokens, LANES), 1) < DH
    zero = jnp.zeros((tokens, LANES), jnp.bfloat16)
    one = jnp.ones((tokens, LANES), jnp.bfloat16)
    ones_two = jnp.concatenate([jnp.where(low, one, zero), jnp.where(low, zero, one)], axis=0)
    for pair in range(width // LANES):
        lanes = slice(pair * LANES, (pair + 1) * LANES)
        keys = key_ref[start : start + tokens, lanes]
        values = value_ref[start : start + tokens, lanes]
        keys_two = jnp.concatenate(
            [jnp.where(low, keys, zero), jnp.where(low, zero, keys)], axis=0
        )
        values_two = jnp.concatenate(
            [jnp.where(low, values, zero), jnp.where(low, zero, values)], axis=0
        )
        scores = lax.dot_general(
            query_ref[place : place + tokens, lanes],
            keys_two,
            (((1,), (1,)), ((), ())),
            preferred_element_type=jnp.float32,
        )
        powers = []
        for h in range(2):
            part = scores[:, h * tokens : (h + 1) * tokens]
            top = jnp.max(part, axis=-1, keepdims=True)
            powers.append(jnp.exp((part - top) * (1.0 / DH**0.5)).astype(jnp.bfloat16))
        powers = jnp.concatenate(powers, axis=1)
        both = dot(powers, jnp.concatenate([values_two, ones_two], axis=1))
        result[place : place + tokens, lanes] = (both[:, :LANES] / both[:, LANES:]).astype(
            jnp.bfloat16
        )


def window_kernel(*refs):
    sources, outs, scratch = refs[:13], refs[13:21], refs[21:]
    far_out, rest_mixed, rest_base, rest_scale, wo, wu, wd = outs[:7]
    gain_refs = (scratch[0], scratch[1], outs[7])
    anchor_ref, count_ref, tok, wq, wk, wv, normed, q_all, k_all, v_all, mixed = scratch[2:13]
    ffn_normed, ffn_hidden, sems = scratch[13:]
    slots, tokens, width = sources[5].shape
    rows = slots * tokens
    cells = tokens // WDEP
    targets = (
        anchor_ref,
        count_ref,
        *gain_refs,
        tok.at[0],
        tok.at[1],
        wq,
        wk,
        wv,
        wo,
        wu,
        wd,
    )
    copies = [
        pltpu.make_async_copy(src, dst, sems.at[i])
        for i, (src, dst) in enumerate(zip(sources, targets, strict=True))
    ]
    for i in (2, 3, 5, 6, 7, 0, 1, 4, 8, 9, 10, 11, 12):
        copies[i].start()
    position = lax.axis_index("brick")
    residue = lax.rem(position, WDEP)

    copies[2].wait()
    copies[3].wait()
    for m in range(2):
        copies[5 + m].wait()
        for s in range(slots):
            start = m * rows + s * tokens
            normed[start : start + tokens, :] = rms_scale(
                tok[m, s].astype(jnp.float32), gain_refs[m][...][None, :]
            )
    for i, (weight, result) in enumerate(((wq, q_all), (wk, k_all), (wv, v_all))):
        copies[7 + i].wait()
        for m in range(2):
            half = slice(m * rows, (m + 1) * rows)
            result[half, :] = dot(normed[half, :], weight[...]).astype(jnp.bfloat16)
    for s in range(slots):
        for m in range(2):
            place, start = m * rows + s * tokens, (1 - m) * rows + s * tokens
            attend(q_all, k_all, v_all, mixed, place, start, tokens)
    for i in (0, 1, 4, 10):
        copies[i].wait()

    def picked(rels):
        places, scales = [], []
        for s in range(slots):
            slot = position * slots + s
            factor = jnp.full((1, LANES), count_ref[slot], jnp.int32).astype(jnp.float32) * (
                1.0 / (2.0 * tokens)
            )
            for rel in rels:
                depth = lax.rem((residue ^ rel) + WDEP * NWRAP - anchor_ref[slot], WDEP)
                places.append((s, depth))
                scales.append(factor * bell_at(depth))
        base, chosen = [], []
        for m in range(2):
            for s, depth in places:
                base.append(tok[m, s, pl.ds(pl.multiple_of(depth * cells, cells), cells), :])
                place = pl.multiple_of(m * rows + s * tokens + depth * cells, cells)
                chosen.append(mixed[pl.ds(place, cells), :])
        return scales, jnp.concatenate(base, axis=0), jnp.concatenate(chosen, axis=0)

    scales, base, chosen = picked((2, 3))
    joined = ffn_rows(
        base,
        chosen,
        gain_refs[2][...][None, :],
        wo,
        wu,
        wd,
        ffn_normed,
        ffn_hidden,
        copies[11].wait,
        copies[12].wait,
    )
    for j, scale in enumerate(scales):
        far_out[(j % 2) * slots + j // 2] = (
            joined[j * cells : (j + 1) * cells] * scale[:, :1]
        ).astype(jnp.bfloat16)
    scales, base, chosen = picked((1, 0))
    rest_base[...] = base
    rest_mixed[...] = chosen
    for j, scale in enumerate(scales):
        rest_scale[j * cells : (j + 1) * cells, :] = jnp.broadcast_to(scale, (cells, LANES))


def near_kernel(
    outer,
    tokens,
    anchor_ref,
    anchor_row,
    count_row,
    rest_mixed,
    rest_base,
    rest_scale,
    wo,
    wu,
    wd,
    gain,
    near_out,
    own_out,
    mask_out,
    bound_out,
    ffn_normed,
    ffn_hidden,
):
    slots, cells, width = near_out.shape
    position = lax.axis_index("brick")
    residue = lax.rem(position, WDEP)
    block = lax.div(position, WDEP)
    joined = ffn_rows(
        rest_base[...],
        rest_mixed[...],
        gain[...][None, :],
        wo,
        wu,
        wd,
        ffn_normed,
        ffn_hidden,
    )
    joined = (joined * rest_scale[:, :1]).astype(jnp.bfloat16)
    for s in range(slots):
        near_out[s] = joined[2 * s * cells : (2 * s + 1) * cells]
        own_out[s] = joined[(2 * s + 1) * cells : (2 * s + 2) * cells]
    for rel in range(WDEP):
        for s in range(slots):
            slot = (block * WDEP + (residue ^ rel)) * slots + s
            start = anchor_ref[slot]
            depth = lax.rem(residue + WDEP * NWRAP - start, WDEP)
            step = lax.div(start + depth, WDEP) ^ block
            for k in range(outer):
                row = k * (WDEP * slots) + rel * slots + s
                mask_out[row : row + 1, :] = jnp.full(
                    (1, LANES), jnp.where(step == k, jnp.float32(1), jnp.float32(0)), jnp.float32
                )
    shift = position - anchor_row[...]
    inside = (shift >= 0) & (shift < WDEP)
    centred = shift.astype(jnp.float32) - (WDEP - 1) / 2.0
    spread = WDEP / 4.0
    terms = (
        count_row[...].astype(jnp.float32)
        / (2.0 * tokens)
        * jnp.exp(-centred * centred / (2.0 * spread * spread))
    )
    bound = jnp.maximum(jnp.sum(jnp.where(inside, terms, 0.0), axis=-1, keepdims=True), 1.0)
    bound_out[...] = jnp.broadcast_to(bound, bound_out.shape)


NWRAP = 1 << 20


def in_hbm(array):
    return pltpu.with_memory_space_constraint(array, pltpu.HBM)


def in_vmem(array):
    return pltpu.with_memory_space_constraint(array, pltpu.VMEM)


def limit(mebibytes):
    return pltpu.CompilerParams(vmem_limit_bytes=mebibytes * 1024 * 1024)


def cost(flops, bytes_accessed):
    return pl.CostEstimate(flops=flops, bytes_accessed=bytes_accessed, transcendentals=0)


def far_call(anchor, count, gains, ct_win, pet_win, weights):
    slots, tokens, width = ct_win.shape
    rows = 2 * slots * tokens
    cells = tokens // WDEP
    half = slots * (WDEP // 2) * cells
    rest = pltpu.VMEM((2 * half, width), jnp.bfloat16)
    big = pltpu.VMEM((rows, width), jnp.bfloat16)
    far, *passed = pl.pallas_call(
        window_kernel,
        out_shape=[
            pltpu.VMEM((2 * slots, cells, width), jnp.bfloat16),
            rest,
            rest,
            pltpu.VMEM((half, LANES), jnp.float32),
        ]
        + [pltpu.VMEM(w.shape, w.dtype) for w in weights[3:]]
        + [pltpu.VMEM((width,), jnp.float32)],
        in_specs=[ANY] * 13,
        out_specs=[VMEM] * 8,
        scratch_shapes=[pltpu.VMEM((width,), jnp.float32)] * 2
        + [pltpu.SMEM(anchor.shape, jnp.int32)] * 2
        + [pltpu.VMEM((2, slots, tokens, width), jnp.bfloat16)]
        + [pltpu.VMEM(w.shape, w.dtype) for w in weights[:3]]
        + [big] * 5
        + [rest, pltpu.VMEM((half, weights[4].shape[1]), jnp.bfloat16)]
        + [pltpu.SemaphoreType.DMA((13,))],
        compiler_params=limit(24),
        name="window_far",
    )(*map(in_hbm, (anchor, count, *gains, ct_win, pet_win, *weights)))
    return far, passed


def near_call(outer, slots, tokens, anchor, count, passed):
    width = passed[0].shape[1]
    cells = tokens // WDEP
    half = slots * (WDEP // 2) * cells
    out = pltpu.VMEM((slots, cells, width), jnp.bfloat16)
    hidden = passed[4].shape[1]
    return pl.pallas_call(
        functools.partial(near_kernel, outer, tokens),
        out_shape=[
            out,
            out,
            pltpu.VMEM((outer * WDEP * slots, LANES), jnp.float32),
            pltpu.VMEM((8, LANES), jnp.float32),
        ],
        in_specs=[SMEM] + [VMEM] * 9,
        out_specs=[VMEM] * 4,
        scratch_shapes=[
            pltpu.VMEM((2 * half, width), jnp.bfloat16),
            pltpu.VMEM((half, hidden), jnp.bfloat16),
        ],
        compiler_params=limit(12),
        cost_estimate=cost(12 * half * width * width, 4 * half * width),
        name="window_near",
    )(in_hbm(anchor), in_hbm(anchor[None, :]), in_hbm(count[None, :]), *map(in_vmem, passed))


def gather_kernel(outer, mask_ref, own, near, far, forward, kept, *sent):
    slots, cells, width = own.shape
    blocks = [own[s] for s in range(slots)] + [near[s] for s in range(slots)]
    blocks += [far[s] for s in range(slots)] + [forward[s] for s in range(slots)]
    blocks = [block.astype(jnp.float32) for block in blocks]
    for k in range(outer):
        total = jnp.zeros((cells, width), jnp.float32)
        for j, block in enumerate(blocks):
            row = k * len(blocks) + j
            mask = jnp.concatenate([mask_ref[row : row + 1, :]] * (width // LANES), axis=1)
            total = total + block * mask
        if k == 0:
            kept[...] = total
        else:
            sent[k - 1][...] = total.astype(jnp.bfloat16)


def gather_call(outer, masks, own, near, far, forward):
    slots, cells, width = own.shape
    return pl.pallas_call(
        functools.partial(gather_kernel, outer),
        out_shape=[pltpu.VMEM((cells, width), jnp.float32)]
        + [pltpu.VMEM((cells, width), jnp.bfloat16)] * (outer - 1),
        in_specs=[VMEM] * 5,
        out_specs=[VMEM] * outer,
        compiler_params=limit(8),
        name="plane_sum",
    )(*map(in_vmem, (masks, own, near, far, forward)))


def upconv_kernel(bound, kept, *refs):
    pieces = refs[:-5]
    weight, up_ref, near_ref, far_ref, grid = refs[-5:]
    channels = up_ref.shape[-1]
    numerator = kept[...]
    for piece in pieces:
        numerator = numerator + piece[...].astype(jnp.float32)
    feature = (numerator / bound[:1, :1]).astype(jnp.bfloat16)
    up_rows = dot(feature, weight[...])
    for a in range(2):
        for b in range(2):
            for c in range(2):
                chunk = (a * 2 + b) * 2 + c
                for y in range(PY):
                    grid[a, 2 * y + b, pl.ds(c, PX, stride=2), :] = up_rows[
                        y * PX : (y + 1) * PX, chunk * channels : (chunk + 1) * channels
                    ]
    upsampled = grid[...].astype(jnp.bfloat16)
    up_ref[...] = upsampled
    even = lax.rem(lax.axis_index("brick"), 2) == 0
    active = jnp.maximum(upsampled, jnp.zeros((), jnp.bfloat16))
    near_ref[...] = jnp.where(even, active[1], active[0])
    far_ref[...] = jnp.where(even, active[0], active[1])


def upconv_call(channels, bound, kept, pieces, weight):
    layer = (2 * PY, 2 * PX, channels)
    return pl.pallas_call(
        upconv_kernel,
        out_shape=[
            pltpu.VMEM((2,) + layer, jnp.bfloat16),
            pltpu.VMEM(layer, jnp.bfloat16),
            pltpu.VMEM(layer, jnp.bfloat16),
        ],
        in_specs=[VMEM] * (3 + len(pieces)),
        out_specs=[VMEM] * 3,
        scratch_shapes=[pltpu.VMEM((2,) + layer, jnp.float32)],
        compiler_params=limit(8),
        name="upconv",
    )(*map(in_vmem, (bound, kept, *pieces, weight)))


def fill_patches(layers, padded, patches):
    height, breadth, channels = layers[0].shape
    rows = height * breadth
    padded[...] = jnp.zeros_like(padded)
    for z, layer in enumerate(layers):
        padded[z, 1 : height + 1, 8 : 8 + breadth, :] = layer.astype(jnp.float32)
    for z in range(len(layers)):
        for dx in range(3):
            column = padded[z, :, 7 + dx : 7 + dx + breadth, :].astype(jnp.bfloat16)
            for dy in range(3):
                tap = dy * 3 + dx
                patches[z * rows : (z + 1) * rows, tap * channels : (tap + 1) * channels] = column[
                    dy : dy + height
                ].reshape(rows, channels)


def conv_local_kernel(up_ref, weight, out_ref, padded, patches):
    depth, height, breadth, channels = up_ref.shape
    rows = height * breadth
    span = 9 * channels
    zero = jnp.zeros((), jnp.bfloat16)
    fill_patches([jnp.maximum(up_ref[z], zero) for z in range(depth)], padded, patches)
    out_ref[...] = up_ref[...].reshape(depth * rows, channels).astype(jnp.float32) + dot(
        patches[...], weight[span : 2 * span, :]
    )
    for z in range(depth - 1):
        out_ref[z * rows : (z + 1) * rows, :] += dot(
            patches[(z + 1) * rows : (z + 2) * rows, :], weight[2 * span :, :]
        )
        out_ref[(z + 1) * rows : (z + 2) * rows, :] += dot(
            patches[z * rows : (z + 1) * rows, :], weight[:span, :]
        )


def conv_halo_kernel(part_ref, near_ref, far_ref, weight, out_ref, padded, patches):
    depth, height, breadth, channels = out_ref.shape
    rows = height * breadth
    span = 9 * channels
    even = lax.rem(lax.axis_index("brick"), 2) == 0
    near, far = near_ref[...], far_ref[...]
    fill_patches([jnp.where(even, far, near), jnp.where(even, near, far)], padded, patches)
    for z in range(depth):
        total = part_ref[z * rows : (z + 1) * rows, :]
        if z == 0:
            total = total + dot(patches[:rows, :], weight[:span, :])
        if z == depth - 1:
            total = total + dot(patches[rows:, :], weight[2 * span :, :])
        out_ref[z] = total.astype(jnp.bfloat16).reshape(height, breadth, channels)


def conv_scratch(depth, height, breadth, channels):
    return [
        pltpu.VMEM((depth, height + 2, breadth + 16, channels), jnp.float32),
        pltpu.VMEM((depth * height * breadth, 9 * channels), jnp.bfloat16),
    ]


def conv_local_call(upsampled, weight):
    depth, height, breadth, channels = upsampled.shape
    rows = depth * height * breadth
    return pl.pallas_call(
        conv_local_kernel,
        out_shape=pltpu.VMEM((rows, channels), jnp.float32),
        in_specs=[VMEM] * 2,
        out_specs=VMEM,
        scratch_shapes=conv_scratch(depth, height, breadth, channels),
        compiler_params=limit(8),
        cost_estimate=cost(36 * rows * channels * channels, 12 * rows * channels),
        name="conv_local",
    )(*map(in_vmem, (upsampled, weight)))


def conv_halo_call(shape, part, near, far, weight):
    return pl.pallas_call(
        conv_halo_kernel,
        out_shape=jax.ShapeDtypeStruct(shape, jnp.bfloat16),
        in_specs=[VMEM] * 4,
        out_specs=VMEM,
        scratch_shapes=conv_scratch(2, *shape[1:]),
        compiler_params=limit(8),
        name="conv_halo",
    )(*map(in_vmem, (part, near, far, weight)))


def swap(values, distance, total):
    return lax.ppermute(values, "brick", [(i, i ^ distance) for i in range(total)])


def on_device(
    ct_win,
    pet_win,
    placed_anchor,
    placed_count,
    norm_ct,
    norm_pet,
    norm_ffn,
    w_query,
    w_key,
    w_value,
    w_out,
    w_up,
    w_down,
    w_upconv,
    w_conv,
):
    slots, tokens, _ = ct_win.shape
    channels = w_conv.shape[1]
    total = lax.axis_size("brick")
    outer = total // WDEP
    far, passed = far_call(
        placed_anchor,
        placed_count,
        (norm_ct, norm_pet, norm_ffn),
        ct_win,
        pet_win,
        (w_query, w_key, w_value, w_out, w_up, w_down),
    )
    far = swap(far, 2, total)
    near, own, masks, bound = near_call(outer, slots, tokens, placed_anchor, placed_count, passed)
    near = swap(near, 1, total)
    forward = swap(far[slots:], 1, total)
    kept, *sent = gather_call(outer, masks, own, near, far, forward)
    pieces = [swap(sent[k - 1], k * WDEP, total) for k in range(outer - 1, 0, -1)]
    upsampled, near, far = upconv_call(channels, bound, kept, pieces, w_upconv)
    pairs = [(i, i + 1) for i in range(1, total - 1, 2)]
    far = lax.ppermute(far, "brick", pairs + [(j, i) for i, j in pairs])
    part = conv_local_call(upsampled, w_conv)
    near, part = lax.optimization_barrier((near, part))
    near = swap(near, 1, total)
    return conv_halo_call(upsampled.shape, part, near, far, w_conv)


def solution(mesh):
    return jax.shard_map(
        on_device,
        mesh=mesh,
        in_specs=(
            P(("groups", "brick"), None, None),
            P(("groups", "brick"), None, None),
            P("groups"),
            P("groups"),
            P(),
            P(),
            P(),
            P(),
            P(),
            P(),
            P(),
            P(),
            P(),
            P(),
            P(),
        ),
        out_specs=P(("groups", "brick"), None, None, None),
        check_vma=False,
    )
```

```python
import functools
import math

import jax
import jax.numpy as jnp
from jax import lax
from jax.experimental import pallas as pl
from jax.experimental.pallas import tpu as pltpu
from jax.sharding import PartitionSpec as P

DH = 64
PY = 4
PX = 8
WDEP = 4
LANES = 128

epsilon = 1e-06

VMEM = pl.BlockSpec(memory_space=pltpu.VMEM)
SMEM = pl.BlockSpec(memory_space=pltpu.SMEM)
ANY = pl.BlockSpec(memory_space=pl.ANY)

BELL = [
    math.exp(-((i - (WDEP - 1) / 2.0) ** 2) / (2.0 * (WDEP / 4.0) ** 2)) for i in range(WDEP)
]


def rms_scale(inputs, gain_vec):
    mean_square = jnp.mean(inputs * inputs, axis=-1, keepdims=True)
    return (inputs * lax.rsqrt(mean_square + epsilon) * gain_vec).astype(jnp.bfloat16)


def dot(left, right):
    return jnp.dot(left, right, preferred_element_type=jnp.float32)


def bell_at(depth):
    value = jnp.float32(BELL[0])
    for i in range(1, WDEP):
        value = jnp.where(depth == i, jnp.float32(BELL[i]), value)
    return value


def ffn_rows(base, mixed, gain_row, wo, wu, wd, normed, hidden, before_up=None, before_down=None):
    half = normed.shape[0] // 2
    total = jnp.zeros((half, normed.shape[1]), jnp.float32)
    for m in range(2):
        rows = slice(m * half, (m + 1) * half)
        mid = base[rows].astype(jnp.float32) + dot(mixed[rows], wo[...])
        normed[rows, :] = rms_scale(mid, gain_row)
        total = total + mid
    if before_up is not None:
        before_up()
    chunk = hidden.shape[1] // 2
    for c in range(2):
        columns = slice(c * chunk, (c + 1) * chunk)
        both = [
            jax.nn.gelu(dot(normed[m * half : (m + 1) * half, :], wu[:, columns]), approximate=True)
            for m in range(2)
        ]
        hidden[:, columns] = (both[0] + both[1]).astype(jnp.bfloat16)
    if before_down is not None:
        before_down()
    return total + dot(hidden[...], wd[...])


def attend(query_ref, key_ref, value_ref, result, place, start, tokens):
    width = query_ref.shape[1]
    low = lax.broadcasted_iota(jnp.int32, (tokens, LANES), 1) < DH
    zero = jnp.zeros((tokens, LANES), jnp.bfloat16)
    one = jnp.ones((tokens, LANES), jnp.bfloat16)
    ones_two = jnp.concatenate([jnp.where(low, one, zero), jnp.where(low, zero, one)], axis=0)
    for pair in range(width // LANES):
        lanes = slice(pair * LANES, (pair + 1) * LANES)
        keys = key_ref[start : start + tokens, lanes]
        values = value_ref[start : start + tokens, lanes]
        keys_two = jnp.concatenate(
            [jnp.where(low, keys, zero), jnp.where(low, zero, keys)], axis=0
        )
        values_two = jnp.concatenate(
            [jnp.where(low, values, zero), jnp.where(low, zero, values)], axis=0
        )
        scores = lax.dot_general(
            query_ref[place : place + tokens, lanes],
            keys_two,
            (((1,), (1,)), ((), ())),
            preferred_element_type=jnp.float32,
        )
        powers = []
        for h in range(2):
            part = scores[:, h * tokens : (h + 1) * tokens]
            top = jnp.max(part, axis=-1, keepdims=True)
            powers.append(jnp.exp((part - top) * (1.0 / DH**0.5)).astype(jnp.bfloat16))
        powers = jnp.concatenate(powers, axis=1)
        both = dot(powers, jnp.concatenate([values_two, ones_two], axis=1))
        result[place : place + tokens, lanes] = (both[:, :LANES] / both[:, LANES:]).astype(
            jnp.bfloat16
        )


def window_kernel(*refs):
    sources, outs, scratch = refs[:13], refs[13:22], refs[22:]
    passing_out, far_out, rest_mixed, rest_base, rest_scale, wo, wu, wd = outs[:8]
    gain_refs = (scratch[0], scratch[1], outs[8])
    anchor_ref, count_ref, tok, wq, wk, wv, normed, q_all, k_all, v_all, mixed = scratch[2:13]
    ffn_normed, ffn_hidden, sems = scratch[13:]
    slots, tokens, width = sources[5].shape
    rows = slots * tokens
    cells = tokens // WDEP
    targets = (
        anchor_ref,
        count_ref,
        *gain_refs,
        tok.at[0],
        tok.at[1],
        wq,
        wk,
        wv,
        wo,
        wu,
        wd,
    )
    copies = [
        pltpu.make_async_copy(src, dst, sems.at[i])
        for i, (src, dst) in enumerate(zip(sources, targets, strict=True))
    ]
    for i in (2, 3, 5, 6, 7, 0, 1, 4, 8, 9, 10, 11, 12):
        copies[i].start()
    position = lax.axis_index("brick")
    residue = lax.rem(position, WDEP)

    copies[2].wait()
    copies[3].wait()
    for m in range(2):
        copies[5 + m].wait()
        for s in range(slots):
            start = m * rows + s * tokens
            normed[start : start + tokens, :] = rms_scale(
                tok[m, s].astype(jnp.float32), gain_refs[m][...][None, :]
            )
    for i, (weight, result) in enumerate(((wq, q_all), (wk, k_all), (wv, v_all))):
        copies[7 + i].wait()
        for m in range(2):
            half = slice(m * rows, (m + 1) * rows)
            result[half, :] = dot(normed[half, :], weight[...]).astype(jnp.bfloat16)
    for s in range(slots):
        for m in range(2):
            place, start = m * rows + s * tokens, (1 - m) * rows + s * tokens
            attend(q_all, k_all, v_all, mixed, place, start, tokens)
    for i in (0, 1, 4, 10):
        copies[i].wait()

    def picked(rels):
        places, scales = [], []
        for s in range(slots):
            slot = position * slots + s
            factor = jnp.full((1, LANES), count_ref[slot], jnp.int32).astype(jnp.float32) * (
                1.0 / (2.0 * tokens)
            )
            for rel in rels:
                depth = lax.rem((residue ^ rel) + WDEP * NWRAP - anchor_ref[slot], WDEP)
                places.append((s, depth))
                scales.append(factor * bell_at(depth))
        base, chosen = [], []
        for m in range(2):
            for s, depth in places:
                base.append(tok[m, s, pl.ds(pl.multiple_of(depth * cells, cells), cells), :])
                place = pl.multiple_of(m * rows + s * tokens + depth * cells, cells)
                chosen.append(mixed[pl.ds(place, cells), :])
        return scales, jnp.concatenate(base, axis=0), jnp.concatenate(chosen, axis=0)

    scales, base, chosen = picked((2, 3))
    joined = ffn_rows(
        base,
        chosen,
        gain_refs[2][...][None, :],
        wo,
        wu,
        wd,
        ffn_normed,
        ffn_hidden,
        copies[11].wait,
        copies[12].wait,
    )
    for j, scale in enumerate(scales):
        out = (far_out, passing_out)[j % 2]
        out[j // 2] = (joined[j * cells : (j + 1) * cells] * scale[:, :1]).astype(jnp.bfloat16)
    scales, base, chosen = picked((1, 0))
    rest_base[...] = base
    rest_mixed[...] = chosen
    for j, scale in enumerate(scales):
        rest_scale[j * cells : (j + 1) * cells, :] = jnp.broadcast_to(scale, (cells, LANES))


def near_kernel(
    outer,
    tokens,
    anchor_ref,
    anchor_row,
    count_row,
    rest_mixed,
    rest_base,
    rest_scale,
    wo,
    wu,
    wd,
    gain,
    near_out,
    own_out,
    mask_out,
    bound_out,
    ffn_normed,
    ffn_hidden,
):
    slots, cells, width = near_out.shape
    position = lax.axis_index("brick")
    residue = lax.rem(position, WDEP)
    block = lax.div(position, WDEP)
    joined = ffn_rows(
        rest_base[...],
        rest_mixed[...],
        gain[...][None, :],
        wo,
        wu,
        wd,
        ffn_normed,
        ffn_hidden,
    )
    joined = (joined * rest_scale[:, :1]).astype(jnp.bfloat16)
    for s in range(slots):
        near_out[s] = joined[2 * s * cells : (2 * s + 1) * cells]
        own_out[s] = joined[(2 * s + 1) * cells : (2 * s + 2) * cells]
    for rel in range(WDEP):
        for s in range(slots):
            slot = (block * WDEP + (residue ^ rel)) * slots + s
            start = anchor_ref[slot]
            depth = lax.rem(residue + WDEP * NWRAP - start, WDEP)
            step = lax.div(start + depth, WDEP) ^ block
            for k in range(outer):
                row = k * (WDEP * slots) + rel * slots + s
                mask_out[row : row + 1, :] = jnp.full(
                    (1, LANES), jnp.where(step == k, jnp.float32(1), jnp.float32(0)), jnp.float32
                )
    shift = position - anchor_row[...]
    inside = (shift >= 0) & (shift < WDEP)
    centred = shift.astype(jnp.float32) - (WDEP - 1) / 2.0
    spread = WDEP / 4.0
    terms = (
        count_row[...].astype(jnp.float32)
        / (2.0 * tokens)
        * jnp.exp(-centred * centred / (2.0 * spread * spread))
    )
    bound = jnp.maximum(jnp.sum(jnp.where(inside, terms, 0.0), axis=-1, keepdims=True), 1.0)
    bound_out[...] = jnp.broadcast_to(bound, bound_out.shape)


NWRAP = 1 << 20


def in_hbm(array):
    return pltpu.with_memory_space_constraint(array, pltpu.HBM)


def in_vmem(array):
    return pltpu.with_memory_space_constraint(array, pltpu.VMEM)


def limit(mebibytes):
    return pltpu.CompilerParams(vmem_limit_bytes=mebibytes * 1024 * 1024)


def cost(flops, bytes_accessed):
    return pl.CostEstimate(flops=flops, bytes_accessed=bytes_accessed, transcendentals=0)


def far_call(anchor, count, gains, ct_win, pet_win, weights):
    slots, tokens, width = ct_win.shape
    rows = 2 * slots * tokens
    cells = tokens // WDEP
    half = slots * (WDEP // 2) * cells
    rest = pltpu.VMEM((2 * half, width), jnp.bfloat16)
    big = pltpu.VMEM((rows, width), jnp.bfloat16)
    out = pltpu.VMEM((slots, cells, width), jnp.bfloat16)
    passing, far, *passed = pl.pallas_call(
        window_kernel,
        out_shape=[
            out,
            out,
            rest,
            rest,
            pltpu.VMEM((half, LANES), jnp.float32),
        ]
        + [pltpu.VMEM(w.shape, w.dtype) for w in weights[3:]]
        + [pltpu.VMEM((width,), jnp.float32)],
        in_specs=[ANY] * 13,
        out_specs=[VMEM] * 9,
        scratch_shapes=[pltpu.VMEM((width,), jnp.float32)] * 2
        + [pltpu.SMEM(anchor.shape, jnp.int32)] * 2
        + [pltpu.VMEM((2, slots, tokens, width), jnp.bfloat16)]
        + [pltpu.VMEM(w.shape, w.dtype) for w in weights[:3]]
        + [big] * 5
        + [rest, pltpu.VMEM((half, weights[4].shape[1]), jnp.bfloat16)]
        + [pltpu.SemaphoreType.DMA((13,))],
        compiler_params=limit(24),
        name="window_far",
    )(*map(in_hbm, (anchor, count, *gains, ct_win, pet_win, *weights)))
    return passing, far, passed


def near_call(outer, slots, tokens, anchor, count, passed):
    width = passed[0].shape[1]
    cells = tokens // WDEP
    half = slots * (WDEP // 2) * cells
    out = pltpu.VMEM((slots, cells, width), jnp.bfloat16)
    hidden = passed[4].shape[1]
    return pl.pallas_call(
        functools.partial(near_kernel, outer, tokens),
        out_shape=[
            out,
            out,
            pltpu.VMEM((outer * WDEP * slots, LANES), jnp.float32),
            pltpu.VMEM((8, LANES), jnp.float32),
        ],
        in_specs=[SMEM] + [VMEM] * 9,
        out_specs=[VMEM] * 4,
        scratch_shapes=[
            pltpu.VMEM((2 * half, width), jnp.bfloat16),
            pltpu.VMEM((half, hidden), jnp.bfloat16),
        ],
        compiler_params=limit(12),
        cost_estimate=cost(12 * half * width * width, 4 * half * width),
        name="window_near",
    )(in_hbm(anchor), in_hbm(anchor[None, :]), in_hbm(count[None, :]), *map(in_vmem, passed))


def gather_kernel(outer, mask_ref, own, near, far, forward, kept, *sent):
    slots, cells, width = own.shape
    blocks = [own[s] for s in range(slots)] + [near[s] for s in range(slots)]
    blocks += [far[s] for s in range(slots)] + [forward[s] for s in range(slots)]
    blocks = [block.astype(jnp.float32) for block in blocks]
    for k in range(outer):
        total = jnp.zeros((cells, width), jnp.float32)
        for j, block in enumerate(blocks):
            row = k * len(blocks) + j
            mask = jnp.concatenate([mask_ref[row : row + 1, :]] * (width // LANES), axis=1)
            total = total + block * mask
        if k == 0:
            kept[...] = total
        else:
            sent[k - 1][...] = total.astype(jnp.bfloat16)


def gather_call(outer, masks, own, near, far, forward):
    slots, cells, width = own.shape
    return pl.pallas_call(
        functools.partial(gather_kernel, outer),
        out_shape=[pltpu.VMEM((cells, width), jnp.float32)]
        + [pltpu.VMEM((cells, width), jnp.bfloat16)] * (outer - 1),
        in_specs=[VMEM] * 5,
        out_specs=[VMEM] * outer,
        compiler_params=limit(8),
        name="plane_sum",
    )(*map(in_vmem, (masks, own, near, far, forward)))


def upconv_kernel(bound, kept, *refs):
    pieces = refs[:-5]
    weight, up_ref, near_ref, far_ref, grid = refs[-5:]
    channels = up_ref.shape[-1]
    numerator = kept[...]
    for piece in pieces:
        numerator = numerator + piece[...].astype(jnp.float32)
    feature = (numerator / bound[:1, :1]).astype(jnp.bfloat16)
    up_rows = dot(feature, weight[...])
    for a in range(2):
        for b in range(2):
            for c in range(2):
                chunk = (a * 2 + b) * 2 + c
                for y in range(PY):
                    grid[a, 2 * y + b, pl.ds(c, PX, stride=2), :] = up_rows[
                        y * PX : (y + 1) * PX, chunk * channels : (chunk + 1) * channels
                    ]
    upsampled = grid[...].astype(jnp.bfloat16)
    up_ref[...] = upsampled
    even = lax.rem(lax.axis_index("brick"), 2) == 0
    active = jnp.maximum(upsampled, jnp.zeros((), jnp.bfloat16))
    near_ref[...] = jnp.where(even, active[1], active[0])
    far_ref[...] = jnp.where(even, active[0], active[1])


def upconv_call(channels, bound, kept, pieces, weight):
    layer = (2 * PY, 2 * PX, channels)
    return pl.pallas_call(
        upconv_kernel,
        out_shape=[
            pltpu.VMEM((2,) + layer, jnp.bfloat16),
            pltpu.VMEM(layer, jnp.bfloat16),
            pltpu.VMEM(layer, jnp.bfloat16),
        ],
        in_specs=[VMEM] * (3 + len(pieces)),
        out_specs=[VMEM] * 3,
        scratch_shapes=[pltpu.VMEM((2,) + layer, jnp.float32)],
        compiler_params=limit(8),
        name="upconv",
    )(*map(in_vmem, (bound, kept, *pieces, weight)))


def fill_patches(layers, padded, patches):
    height, breadth, channels = layers[0].shape
    rows = height * breadth
    padded[...] = jnp.zeros_like(padded)
    for z, layer in enumerate(layers):
        padded[z, 1 : height + 1, 8 : 8 + breadth, :] = layer.astype(jnp.float32)
    for z in range(len(layers)):
        for dx in range(3):
            column = padded[z, :, 7 + dx : 7 + dx + breadth, :].astype(jnp.bfloat16)
            for dy in range(3):
                tap = dy * 3 + dx
                patches[z * rows : (z + 1) * rows, tap * channels : (tap + 1) * channels] = column[
                    dy : dy + height
                ].reshape(rows, channels)


def conv_local_kernel(up_ref, weight, out_ref, padded, patches):
    depth, height, breadth, channels = up_ref.shape
    rows = height * breadth
    span = 9 * channels
    zero = jnp.zeros((), jnp.bfloat16)
    fill_patches([jnp.maximum(up_ref[z], zero) for z in range(depth)], padded, patches)
    out_ref[...] = up_ref[...].reshape(depth * rows, channels).astype(jnp.float32) + dot(
        patches[...], weight[span : 2 * span, :]
    )
    for z in range(depth - 1):
        out_ref[z * rows : (z + 1) * rows, :] += dot(
            patches[(z + 1) * rows : (z + 2) * rows, :], weight[2 * span :, :]
        )
        out_ref[(z + 1) * rows : (z + 2) * rows, :] += dot(
            patches[z * rows : (z + 1) * rows, :], weight[:span, :]
        )


def conv_halo_kernel(part_ref, near_ref, far_ref, weight, out_ref, padded, patches):
    depth, height, breadth, channels = out_ref.shape
    rows = height * breadth
    span = 9 * channels
    even = lax.rem(lax.axis_index("brick"), 2) == 0
    near, far = near_ref[...], far_ref[...]
    fill_patches([jnp.where(even, far, near), jnp.where(even, near, far)], padded, patches)
    for z in range(depth):
        total = part_ref[z * rows : (z + 1) * rows, :]
        if z == 0:
            total = total + dot(patches[:rows, :], weight[:span, :])
        if z == depth - 1:
            total = total + dot(patches[rows:, :], weight[2 * span :, :])
        out_ref[z] = total.astype(jnp.bfloat16).reshape(height, breadth, channels)


def conv_scratch(depth, height, breadth, channels):
    return [
        pltpu.VMEM((depth, height + 2, breadth + 16, channels), jnp.float32),
        pltpu.VMEM((depth * height * breadth, 9 * channels), jnp.bfloat16),
    ]


def conv_local_call(upsampled, weight):
    depth, height, breadth, channels = upsampled.shape
    rows = depth * height * breadth
    return pl.pallas_call(
        conv_local_kernel,
        out_shape=pltpu.VMEM((rows, channels), jnp.float32),
        in_specs=[VMEM] * 2,
        out_specs=VMEM,
        scratch_shapes=conv_scratch(depth, height, breadth, channels),
        compiler_params=limit(8),
        cost_estimate=cost(36 * rows * channels * channels, 12 * rows * channels),
        name="conv_local",
    )(*map(in_vmem, (upsampled, weight)))


def conv_halo_call(shape, part, near, far, weight):
    return pl.pallas_call(
        conv_halo_kernel,
        out_shape=jax.ShapeDtypeStruct(shape, jnp.bfloat16),
        in_specs=[VMEM] * 4,
        out_specs=VMEM,
        scratch_shapes=conv_scratch(2, *shape[1:]),
        compiler_params=limit(8),
        name="conv_halo",
    )(*map(in_vmem, (part, near, far, weight)))


def swap(values, distance, total):
    return lax.ppermute(values, "brick", [(i, i ^ distance) for i in range(total)])


def on_device(
    ct_win,
    pet_win,
    placed_anchor,
    placed_count,
    norm_ct,
    norm_pet,
    norm_ffn,
    w_query,
    w_key,
    w_value,
    w_out,
    w_up,
    w_down,
    w_upconv,
    w_conv,
):
    slots, tokens, _ = ct_win.shape
    channels = w_conv.shape[1]
    total = lax.axis_size("brick")
    outer = total // WDEP
    passing, far, passed = far_call(
        placed_anchor,
        placed_count,
        (norm_ct, norm_pet, norm_ffn),
        ct_win,
        pet_win,
        (w_query, w_key, w_value, w_out, w_up, w_down),
    )
    far = swap(far, 2, total)
    passing = swap(passing, 3, total)
    near, own, masks, bound = near_call(outer, slots, tokens, placed_anchor, placed_count, passed)
    near, far = lax.optimization_barrier((near, far))
    near = swap(near, 1, total)
    kept, *sent = gather_call(outer, masks, own, near, far, passing)
    pieces = [swap(sent[k - 1], k * WDEP, total) for k in range(outer - 1, 0, -1)]
    upsampled, near, far = upconv_call(channels, bound, kept, pieces, w_upconv)
    pairs = [(i, i + 1) for i in range(1, total - 1, 2)]
    far = lax.ppermute(far, "brick", pairs + [(j, i) for i, j in pairs])
    part = conv_local_call(upsampled, w_conv)
    near, part = lax.optimization_barrier((near, part))
    near = swap(near, 1, total)
    return conv_halo_call(upsampled.shape, part, near, far, w_conv)


def solution(mesh):
    return jax.shard_map(
        on_device,
        mesh=mesh,
        in_specs=(
            P(("groups", "brick"), None, None),
            P(("groups", "brick"), None, None),
            P("groups"),
            P("groups"),
            P(),
            P(),
            P(),
            P(),
            P(),
            P(),
            P(),
            P(),
            P(),
            P(),
            P(),
        ),
        out_specs=P(("groups", "brick"), None, None, None),
        check_vma=False,
    )
```

```python
import functools
import math

import jax
import jax.numpy as jnp
from jax import lax
from jax.experimental import pallas as pl
from jax.experimental.pallas import tpu as pltpu
from jax.sharding import PartitionSpec as P

DH = 64
PY = 4
PX = 8
WDEP = 4
LANES = 128

epsilon = 1e-06

VMEM = pl.BlockSpec(memory_space=pltpu.VMEM)
SMEM = pl.BlockSpec(memory_space=pltpu.SMEM)
ANY = pl.BlockSpec(memory_space=pl.ANY)

BELL = [
    math.exp(-((i - (WDEP - 1) / 2.0) ** 2) / (2.0 * (WDEP / 4.0) ** 2)) for i in range(WDEP)
]


def rms_scale(inputs, gain_vec):
    mean_square = jnp.mean(inputs * inputs, axis=-1, keepdims=True)
    return (inputs * lax.rsqrt(mean_square + epsilon) * gain_vec).astype(jnp.bfloat16)


def dot(left, right):
    return jnp.dot(left, right, preferred_element_type=jnp.float32)


def bell_at(depth):
    value = jnp.float32(BELL[0])
    for i in range(1, WDEP):
        value = jnp.where(depth == i, jnp.float32(BELL[i]), value)
    return value


def ffn_rows(base, mixed, gain_row, wo, wu, wd, normed, hidden):
    half = normed.shape[0] // 2
    total = jnp.zeros((half, normed.shape[1]), jnp.float32)
    for m in range(2):
        rows = slice(m * half, (m + 1) * half)
        mid = base[rows].astype(jnp.float32) + dot(mixed[rows], wo[...])
        normed[rows, :] = rms_scale(mid, gain_row)
        total = total + mid
    chunk = hidden.shape[1] // 2
    for c in range(2):
        columns = slice(c * chunk, (c + 1) * chunk)
        both = [
            jax.nn.gelu(dot(normed[m * half : (m + 1) * half, :], wu[:, columns]), approximate=True)
            for m in range(2)
        ]
        hidden[:, columns] = (both[0] + both[1]).astype(jnp.bfloat16)
    return total + dot(hidden[...], wd[...])


def attend(query_ref, key_ref, value_ref, result, place, start, tokens):
    width = query_ref.shape[1]
    low = lax.broadcasted_iota(jnp.int32, (tokens, LANES), 1) < DH
    zero = jnp.zeros((tokens, LANES), jnp.bfloat16)
    one = jnp.ones((tokens, LANES), jnp.bfloat16)
    ones_two = jnp.concatenate([jnp.where(low, one, zero), jnp.where(low, zero, one)], axis=0)
    for pair in range(width // LANES):
        lanes = slice(pair * LANES, (pair + 1) * LANES)
        keys = key_ref[start : start + tokens, lanes]
        values = value_ref[start : start + tokens, lanes]
        keys_two = jnp.concatenate(
            [jnp.where(low, keys, zero), jnp.where(low, zero, keys)], axis=0
        )
        values_two = jnp.concatenate(
            [jnp.where(low, values, zero), jnp.where(low, zero, values)], axis=0
        )
        scores = lax.dot_general(
            query_ref[place : place + tokens, lanes],
            keys_two,
            (((1,), (1,)), ((), ())),
            preferred_element_type=jnp.float32,
        )
        powers = []
        for h in range(2):
            part = scores[:, h * tokens : (h + 1) * tokens]
            top = jnp.max(part, axis=-1, keepdims=True)
            powers.append(jnp.exp((part - top) * (1.0 / DH**0.5)).astype(jnp.bfloat16))
        powers = jnp.concatenate(powers, axis=1)
        both = dot(powers, jnp.concatenate([values_two, ones_two], axis=1))
        result[place : place + tokens, lanes] = (both[:, :LANES] / both[:, LANES:]).astype(
            jnp.bfloat16
        )


def window_kernel(*refs):
    sources, outs, scratch = refs[:13], refs[13:22], refs[22:]
    passing_out, far_out, rest_mixed, rest_base, rest_scale, wo, wu, wd = outs[:8]
    gain_refs = (scratch[0], scratch[1], outs[8])
    anchor_ref, count_ref, tok, wq, wk, wv, normed, q_all, k_all, v_all, mixed = scratch[2:13]
    ffn_normed, ffn_hidden, sems = scratch[13:]
    slots, tokens, width = sources[5].shape
    rows = slots * tokens
    cells = tokens // WDEP
    targets = (
        anchor_ref,
        count_ref,
        *gain_refs,
        tok.at[0],
        tok.at[1],
        wq,
        wk,
        wv,
        wo,
        wu,
        wd,
    )
    copies = [
        pltpu.make_async_copy(src, dst, sems.at[i])
        for i, (src, dst) in enumerate(zip(sources, targets, strict=True))
    ]
    for i in (5, 2, 6, 3, 7, 8, 9, 10, 11, 12, 0, 1, 4):
        copies[i].start()
    position = lax.axis_index("brick")
    residue = lax.rem(position, WDEP)

    copies[2].wait()
    copies[3].wait()
    for m in range(2):
        copies[5 + m].wait()
        for s in range(slots):
            start = m * rows + s * tokens
            normed[start : start + tokens, :] = rms_scale(
                tok[m, s].astype(jnp.float32), gain_refs[m][...][None, :]
            )
    for i, (weight, result) in enumerate(((wq, q_all), (wk, k_all), (wv, v_all))):
        for n in ((7,), (8, 9), ())[i]:
            copies[n].wait()
        for m in range(2):
            half = slice(m * rows, (m + 1) * rows)
            result[half, :] = dot(normed[half, :], weight[...]).astype(jnp.bfloat16)
    for s in range(slots):
        for m in range(2):
            place, start = m * rows + s * tokens, (1 - m) * rows + s * tokens
            attend(q_all, k_all, v_all, mixed, place, start, tokens)
    for i in (0, 1, 4, 10, 11, 12):
        copies[i].wait()

    def picked(rels):
        places, scales = [], []
        for s in range(slots):
            slot = position * slots + s
            factor = jnp.full((1, LANES), count_ref[slot], jnp.int32).astype(jnp.float32) * (
                1.0 / (2.0 * tokens)
            )
            for rel in rels:
                depth = lax.rem((residue ^ rel) + WDEP * NWRAP - anchor_ref[slot], WDEP)
                places.append((s, depth))
                scales.append(factor * bell_at(depth))
        base, chosen = [], []
        for m in range(2):
            for s, depth in places:
                base.append(tok[m, s, pl.ds(pl.multiple_of(depth * cells, cells), cells), :])
                place = pl.multiple_of(m * rows + s * tokens + depth * cells, cells)
                chosen.append(mixed[pl.ds(place, cells), :])
        return scales, jnp.concatenate(base, axis=0), jnp.concatenate(chosen, axis=0)

    scales, base, chosen = picked((2, 3))
    joined = ffn_rows(
        base,
        chosen,
        gain_refs[2][...][None, :],
        wo,
        wu,
        wd,
        ffn_normed,
        ffn_hidden,
    )
    for j, scale in enumerate(scales):
        out = (far_out, passing_out)[j % 2]
        out[j // 2] = (joined[j * cells : (j + 1) * cells] * scale[:, :1]).astype(jnp.bfloat16)
    scales, base, chosen = picked((1, 0))
    rest_base[...] = base
    rest_mixed[...] = chosen
    for j, scale in enumerate(scales):
        rest_scale[j * cells : (j + 1) * cells, :] = jnp.broadcast_to(scale, (cells, LANES))


def near_kernel(
    outer,
    tokens,
    anchor_ref,
    anchor_row,
    count_row,
    rest_mixed,
    rest_base,
    rest_scale,
    wo,
    wu,
    wd,
    gain,
    near_out,
    own_out,
    mask_out,
    bound_out,
    ffn_normed,
    ffn_hidden,
):
    slots, cells, width = near_out.shape
    position = lax.axis_index("brick")
    residue = lax.rem(position, WDEP)
    block = lax.div(position, WDEP)
    joined = ffn_rows(
        rest_base[...],
        rest_mixed[...],
        gain[...][None, :],
        wo,
        wu,
        wd,
        ffn_normed,
        ffn_hidden,
    )
    joined = (joined * rest_scale[:, :1]).astype(jnp.bfloat16)
    for s in range(slots):
        near_out[s] = joined[2 * s * cells : (2 * s + 1) * cells]
        own_out[s] = joined[(2 * s + 1) * cells : (2 * s + 2) * cells]
    for rel in range(WDEP):
        for s in range(slots):
            slot = (block * WDEP + (residue ^ rel)) * slots + s
            start = anchor_ref[slot]
            depth = lax.rem(residue + WDEP * NWRAP - start, WDEP)
            step = lax.div(start + depth, WDEP) ^ block
            for k in range(outer):
                row = k * (WDEP * slots) + rel * slots + s
                mask_out[row : row + 1, :] = jnp.full(
                    (1, LANES), jnp.where(step == k, jnp.float32(1), jnp.float32(0)), jnp.float32
                )
    shift = position - anchor_row[...]
    inside = (shift >= 0) & (shift < WDEP)
    centred = shift.astype(jnp.float32) - (WDEP - 1) / 2.0
    spread = WDEP / 4.0
    terms = (
        count_row[...].astype(jnp.float32)
        / (2.0 * tokens)
        * jnp.exp(-centred * centred / (2.0 * spread * spread))
    )
    bound = jnp.maximum(jnp.sum(jnp.where(inside, terms, 0.0), axis=-1, keepdims=True), 1.0)
    bound_out[...] = jnp.broadcast_to(bound, bound_out.shape)


NWRAP = 1 << 20


def in_hbm(array):
    return pltpu.with_memory_space_constraint(array, pltpu.HBM)


def in_vmem(array):
    return pltpu.with_memory_space_constraint(array, pltpu.VMEM)


def limit(mebibytes):
    return pltpu.CompilerParams(vmem_limit_bytes=mebibytes * 1024 * 1024)


def cost(flops, bytes_accessed):
    return pl.CostEstimate(flops=flops, bytes_accessed=bytes_accessed, transcendentals=0)


def far_call(anchor, count, gains, ct_win, pet_win, weights):
    slots, tokens, width = ct_win.shape
    rows = 2 * slots * tokens
    cells = tokens // WDEP
    half = slots * (WDEP // 2) * cells
    rest = pltpu.VMEM((2 * half, width), jnp.bfloat16)
    big = pltpu.VMEM((rows, width), jnp.bfloat16)
    out = pltpu.VMEM((slots, cells, width), jnp.bfloat16)
    passing, far, *passed = pl.pallas_call(
        window_kernel,
        out_shape=[
            out,
            out,
            rest,
            rest,
            pltpu.VMEM((half, LANES), jnp.float32),
        ]
        + [pltpu.VMEM(w.shape, w.dtype) for w in weights[3:]]
        + [pltpu.VMEM((width,), jnp.float32)],
        in_specs=[ANY] * 13,
        out_specs=[VMEM] * 9,
        scratch_shapes=[pltpu.VMEM((width,), jnp.float32)] * 2
        + [pltpu.SMEM(anchor.shape, jnp.int32)] * 2
        + [pltpu.VMEM((2, slots, tokens, width), jnp.bfloat16)]
        + [pltpu.VMEM(w.shape, w.dtype) for w in weights[:3]]
        + [big] * 5
        + [rest, pltpu.VMEM((half, weights[4].shape[1]), jnp.bfloat16)]
        + [pltpu.SemaphoreType.DMA((13,))],
        compiler_params=limit(24),
        name="window_far",
    )(*map(in_hbm, (anchor, count, *gains, ct_win, pet_win, *weights)))
    return passing, far, passed


def near_call(outer, slots, tokens, anchor, count, passed):
    width = passed[0].shape[1]
    cells = tokens // WDEP
    half = slots * (WDEP // 2) * cells
    out = pltpu.VMEM((slots, cells, width), jnp.bfloat16)
    hidden = passed[4].shape[1]
    return pl.pallas_call(
        functools.partial(near_kernel, outer, tokens),
        out_shape=[
            out,
            out,
            pltpu.VMEM((outer * WDEP * slots, LANES), jnp.float32),
            pltpu.VMEM((8, LANES), jnp.float32),
        ],
        in_specs=[SMEM] + [VMEM] * 9,
        out_specs=[VMEM] * 4,
        scratch_shapes=[
            pltpu.VMEM((2 * half, width), jnp.bfloat16),
            pltpu.VMEM((half, hidden), jnp.bfloat16),
        ],
        compiler_params=limit(12),
        cost_estimate=cost(12 * half * width * width, 4 * half * width),
        name="window_near",
    )(in_hbm(anchor), in_hbm(anchor[None, :]), in_hbm(count[None, :]), *map(in_vmem, passed))


def gather_kernel(outer, mask_ref, own, near, far, forward, kept, *sent):
    slots, cells, width = own.shape
    blocks = [own[s] for s in range(slots)] + [near[s] for s in range(slots)]
    blocks += [far[s] for s in range(slots)] + [forward[s] for s in range(slots)]
    blocks = [block.astype(jnp.float32) for block in blocks]
    for k in range(outer):
        total = jnp.zeros((cells, width), jnp.float32)
        for j, block in enumerate(blocks):
            row = k * len(blocks) + j
            mask = jnp.concatenate([mask_ref[row : row + 1, :]] * (width // LANES), axis=1)
            total = total + block * mask
        if k == 0:
            kept[...] = total
        else:
            sent[k - 1][...] = total.astype(jnp.bfloat16)


def gather_call(outer, masks, own, near, far, forward):
    slots, cells, width = own.shape
    return pl.pallas_call(
        functools.partial(gather_kernel, outer),
        out_shape=[pltpu.VMEM((cells, width), jnp.float32)]
        + [pltpu.VMEM((cells, width), jnp.bfloat16)] * (outer - 1),
        in_specs=[VMEM] * 5,
        out_specs=[VMEM] * outer,
        compiler_params=limit(8),
        name="plane_sum",
    )(*map(in_vmem, (masks, own, near, far, forward)))


def upconv_kernel(bound, kept, *refs):
    pieces = refs[:-5]
    weight, up_ref, near_ref, far_ref, grid = refs[-5:]
    channels = up_ref.shape[-1]
    numerator = kept[...]
    for piece in pieces:
        numerator = numerator + piece[...].astype(jnp.float32)
    feature = (numerator / bound[:1, :1]).astype(jnp.bfloat16)
    up_rows = dot(feature, weight[...])
    for a in range(2):
        for b in range(2):
            for c in range(2):
                chunk = (a * 2 + b) * 2 + c
                for y in range(PY):
                    grid[a, 2 * y + b, pl.ds(c, PX, stride=2), :] = up_rows[
                        y * PX : (y + 1) * PX, chunk * channels : (chunk + 1) * channels
                    ]
    upsampled = grid[...].astype(jnp.bfloat16)
    up_ref[...] = upsampled
    even = lax.rem(lax.axis_index("brick"), 2) == 0
    active = jnp.maximum(upsampled, jnp.zeros((), jnp.bfloat16))
    near_ref[...] = jnp.where(even, active[1], active[0])
    far_ref[...] = jnp.where(even, active[0], active[1])


def upconv_call(channels, bound, kept, pieces, weight):
    layer = (2 * PY, 2 * PX, channels)
    return pl.pallas_call(
        upconv_kernel,
        out_shape=[
            pltpu.VMEM((2,) + layer, jnp.bfloat16),
            pltpu.VMEM(layer, jnp.bfloat16),
            pltpu.VMEM(layer, jnp.bfloat16),
        ],
        in_specs=[VMEM] * (3 + len(pieces)),
        out_specs=[VMEM] * 3,
        scratch_shapes=[pltpu.VMEM((2,) + layer, jnp.float32)],
        compiler_params=limit(8),
        name="upconv",
    )(*map(in_vmem, (bound, kept, *pieces, weight)))


def fill_patches(layers, padded, patches):
    height, breadth, channels = layers[0].shape
    rows = height * breadth
    padded[...] = jnp.zeros_like(padded)
    for z, layer in enumerate(layers):
        padded[z, 1 : height + 1, 8 : 8 + breadth, :] = layer.astype(jnp.float32)
    for z in range(len(layers)):
        for dx in range(3):
            column = padded[z, :, 7 + dx : 7 + dx + breadth, :].astype(jnp.bfloat16)
            for dy in range(3):
                tap = dy * 3 + dx
                patches[z * rows : (z + 1) * rows, tap * channels : (tap + 1) * channels] = column[
                    dy : dy + height
                ].reshape(rows, channels)


def conv_local_kernel(up_ref, weight, out_ref, padded, patches):
    depth, height, breadth, channels = up_ref.shape
    rows = height * breadth
    span = 9 * channels
    zero = jnp.zeros((), jnp.bfloat16)
    fill_patches([jnp.maximum(up_ref[z], zero) for z in range(depth)], padded, patches)
    out_ref[...] = up_ref[...].reshape(depth * rows, channels).astype(jnp.float32) + dot(
        patches[...], weight[span : 2 * span, :]
    )
    for z in range(depth - 1):
        out_ref[z * rows : (z + 1) * rows, :] += dot(
            patches[(z + 1) * rows : (z + 2) * rows, :], weight[2 * span :, :]
        )
        out_ref[(z + 1) * rows : (z + 2) * rows, :] += dot(
            patches[z * rows : (z + 1) * rows, :], weight[:span, :]
        )


def conv_halo_kernel(part_ref, near_ref, far_ref, weight, out_ref, padded, patches):
    depth, height, breadth, channels = out_ref.shape
    rows = height * breadth
    span = 9 * channels
    even = lax.rem(lax.axis_index("brick"), 2) == 0
    near, far = near_ref[...], far_ref[...]
    fill_patches([jnp.where(even, far, near), jnp.where(even, near, far)], padded, patches)
    for z in range(depth):
        total = part_ref[z * rows : (z + 1) * rows, :]
        if z == 0:
            total = total + dot(patches[:rows, :], weight[:span, :])
        if z == depth - 1:
            total = total + dot(patches[rows:, :], weight[2 * span :, :])
        out_ref[z] = total.astype(jnp.bfloat16).reshape(height, breadth, channels)


def conv_scratch(depth, height, breadth, channels):
    return [
        pltpu.VMEM((depth, height + 2, breadth + 16, channels), jnp.float32),
        pltpu.VMEM((depth * height * breadth, 9 * channels), jnp.bfloat16),
    ]


def conv_local_call(upsampled, weight):
    depth, height, breadth, channels = upsampled.shape
    rows = depth * height * breadth
    return pl.pallas_call(
        conv_local_kernel,
        out_shape=pltpu.VMEM((rows, channels), jnp.float32),
        in_specs=[VMEM] * 2,
        out_specs=VMEM,
        scratch_shapes=conv_scratch(depth, height, breadth, channels),
        compiler_params=limit(8),
        cost_estimate=cost(36 * rows * channels * channels, 12 * rows * channels),
        name="conv_local",
    )(*map(in_vmem, (upsampled, weight)))


def conv_halo_call(shape, part, near, far, weight):
    return pl.pallas_call(
        conv_halo_kernel,
        out_shape=jax.ShapeDtypeStruct(shape, jnp.bfloat16),
        in_specs=[VMEM] * 4,
        out_specs=VMEM,
        scratch_shapes=conv_scratch(2, *shape[1:]),
        compiler_params=limit(8),
        name="conv_halo",
    )(*map(in_vmem, (part, near, far, weight)))


def swap(values, distance, total):
    return lax.ppermute(values, "brick", [(i, i ^ distance) for i in range(total)])


def on_device(
    ct_win,
    pet_win,
    placed_anchor,
    placed_count,
    norm_ct,
    norm_pet,
    norm_ffn,
    w_query,
    w_key,
    w_value,
    w_out,
    w_up,
    w_down,
    w_upconv,
    w_conv,
):
    slots, tokens, _ = ct_win.shape
    channels = w_conv.shape[1]
    total = lax.axis_size("brick")
    outer = total // WDEP
    passing, far, passed = far_call(
        placed_anchor,
        placed_count,
        (norm_ct, norm_pet, norm_ffn),
        ct_win,
        pet_win,
        (w_query, w_key, w_value, w_out, w_up, w_down),
    )
    far = swap(far, 2, total)
    passing = swap(passing, 3, total)
    near, own, masks, bound = near_call(outer, slots, tokens, placed_anchor, placed_count, passed)
    near, far = lax.optimization_barrier((near, far))
    near = swap(near, 1, total)
    kept, *sent = gather_call(outer, masks, own, near, far, passing)
    pieces = [swap(sent[k - 1], k * WDEP, total) for k in range(outer - 1, 0, -1)]
    upsampled, near, far = upconv_call(channels, bound, kept, pieces, w_upconv)
    pairs = [(i, i + 1) for i in range(1, total - 1, 2)]
    far = lax.ppermute(far, "brick", pairs + [(j, i) for i, j in pairs])
    part = conv_local_call(upsampled, w_conv)
    near, part = lax.optimization_barrier((near, part))
    near = swap(near, 1, total)
    return conv_halo_call(upsampled.shape, part, near, far, w_conv)


def solution(mesh):
    return jax.shard_map(
        on_device,
        mesh=mesh,
        in_specs=(
            P(("groups", "brick"), None, None),
            P(("groups", "brick"), None, None),
            P("groups"),
            P("groups"),
            P(),
            P(),
            P(),
            P(),
            P(),
            P(),
            P(),
            P(),
            P(),
            P(),
            P(),
        ),
        out_specs=P(("groups", "brick"), None, None, None),
        check_vma=False,
    )
```

```python
import functools
import math

import jax
import jax.numpy as jnp
from jax import lax
from jax.experimental import pallas as pl
from jax.experimental.pallas import tpu as pltpu
from jax.sharding import PartitionSpec as P

DH = 64
PY = 4
PX = 8
WDEP = 4
LANES = 128

epsilon = 1e-06

VMEM = pl.BlockSpec(memory_space=pltpu.VMEM)
SMEM = pl.BlockSpec(memory_space=pltpu.SMEM)
ANY = pl.BlockSpec(memory_space=pl.ANY)

BELL = [
    math.exp(-((i - (WDEP - 1) / 2.0) ** 2) / (2.0 * (WDEP / 4.0) ** 2)) for i in range(WDEP)
]


def rms_scale(inputs, gain_vec):
    mean_square = jnp.mean(inputs * inputs, axis=-1, keepdims=True)
    return (inputs * lax.rsqrt(mean_square + epsilon) * gain_vec).astype(jnp.bfloat16)


def dot(left, right):
    return jnp.dot(left, right, preferred_element_type=jnp.float32)


def bell_at(depth):
    value = jnp.float32(BELL[0])
    for i in range(1, WDEP):
        value = jnp.where(depth == i, jnp.float32(BELL[i]), value)
    return value


def ffn_rows(base, mixed, gain_row, wo, wu, wd, normed, hidden):
    half = normed.shape[0] // 2
    total = jnp.zeros((half, normed.shape[1]), jnp.float32)
    for m in range(2):
        rows = slice(m * half, (m + 1) * half)
        mid = base[rows].astype(jnp.float32) + dot(mixed[rows], wo[...])
        normed[rows, :] = rms_scale(mid, gain_row)
        total = total + mid
    chunk = hidden.shape[1] // 2
    for c in range(2):
        columns = slice(c * chunk, (c + 1) * chunk)
        both = [
            jax.nn.gelu(dot(normed[m * half : (m + 1) * half, :], wu[:, columns]), approximate=True)
            for m in range(2)
        ]
        hidden[:, columns] = (both[0] + both[1]).astype(jnp.bfloat16)
    return total + dot(hidden[...], wd[...])


def attend(query_ref, key_ref, value_ref, result, place, start, tokens):
    width = query_ref.shape[1]
    low = lax.broadcasted_iota(jnp.int32, (tokens, LANES), 1) < DH
    zero = jnp.zeros((tokens, LANES), jnp.bfloat16)
    one = jnp.ones((tokens, LANES), jnp.bfloat16)
    ones_two = jnp.concatenate([jnp.where(low, one, zero), jnp.where(low, zero, one)], axis=0)
    for pair in range(width // LANES):
        lanes = slice(pair * LANES, (pair + 1) * LANES)
        keys = key_ref[start : start + tokens, lanes]
        values = value_ref[start : start + tokens, lanes]
        keys_two = jnp.concatenate(
            [jnp.where(low, keys, zero), jnp.where(low, zero, keys)], axis=0
        )
        values_two = jnp.concatenate(
            [jnp.where(low, values, zero), jnp.where(low, zero, values)], axis=0
        )
        scores = lax.dot_general(
            query_ref[place : place + tokens, lanes],
            keys_two,
            (((1,), (1,)), ((), ())),
            preferred_element_type=jnp.float32,
        )
        powers = []
        for h in range(2):
            part = scores[:, h * tokens : (h + 1) * tokens]
            top = jnp.max(part, axis=-1, keepdims=True)
            powers.append(jnp.exp((part - top) * (1.0 / DH**0.5)).astype(jnp.bfloat16))
        powers = jnp.concatenate(powers, axis=1)
        both = dot(powers, jnp.concatenate([values_two, ones_two], axis=1))
        result[place : place + tokens, lanes] = (both[:, :LANES] / both[:, LANES:]).astype(
            jnp.bfloat16
        )


def window_kernel(*refs):
    sources, outs, scratch = refs[:13], refs[13:22], refs[22:]
    passing_out, far_out, rest_mixed, rest_base, rest_scale, wo, wu, wd = outs[:8]
    gain_refs = (scratch[0], scratch[1], outs[8])
    anchor_ref, count_ref, tok, wq, wk, wv, normed, q_all, k_all, v_all, mixed = scratch[2:13]
    ffn_normed, ffn_hidden, sems = scratch[13:]
    slots, tokens, width = sources[5].shape
    rows = slots * tokens
    cells = tokens // WDEP
    targets = (
        anchor_ref,
        count_ref,
        *gain_refs,
        tok.at[0],
        tok.at[1],
        wq,
        wk,
        wv,
        wo,
        wu,
        wd,
    )
    copies = [
        pltpu.make_async_copy(src, dst, sems.at[i])
        for i, (src, dst) in enumerate(zip(sources, targets, strict=True))
    ]
    for i in (5, 2, 6, 3, 7, 8, 9, 10, 11, 12, 0, 1, 4):
        copies[i].start()
    position = lax.axis_index("brick")
    residue = lax.rem(position, WDEP)

    copies[2].wait()
    copies[3].wait()
    for m in range(2):
        copies[5 + m].wait()
        for s in range(slots):
            start = m * rows + s * tokens
            normed[start : start + tokens, :] = rms_scale(
                tok[m, s].astype(jnp.float32), gain_refs[m][...][None, :]
            )
    for i, (weight, result) in enumerate(((wq, q_all), (wk, k_all), (wv, v_all))):
        for n in ((7,), (8, 9), ())[i]:
            copies[n].wait()
        for m in range(2):
            half = slice(m * rows, (m + 1) * rows)
            result[half, :] = dot(normed[half, :], weight[...]).astype(jnp.bfloat16)
    for s in range(slots):
        for m in range(2):
            place, start = m * rows + s * tokens, (1 - m) * rows + s * tokens
            attend(q_all, k_all, v_all, mixed, place, start, tokens)
    for i in (0, 1, 4, 10, 11, 12):
        copies[i].wait()

    def picked(rels):
        places, scales = [], []
        for s in range(slots):
            slot = position * slots + s
            factor = jnp.full((1, LANES), count_ref[slot], jnp.int32).astype(jnp.float32) * (
                1.0 / (2.0 * tokens)
            )
            for rel in rels:
                depth = lax.rem((residue ^ rel) + WDEP * NWRAP - anchor_ref[slot], WDEP)
                places.append((s, depth))
                scales.append(factor * bell_at(depth))
        base, chosen = [], []
        for m in range(2):
            for s, depth in places:
                base.append(tok[m, s, pl.ds(pl.multiple_of(depth * cells, cells), cells), :])
                place = pl.multiple_of(m * rows + s * tokens + depth * cells, cells)
                chosen.append(mixed[pl.ds(place, cells), :])
        return scales, jnp.concatenate(base, axis=0), jnp.concatenate(chosen, axis=0)

    scales, base, chosen = picked((2, 3))
    joined = ffn_rows(
        base,
        chosen,
        gain_refs[2][...][None, :],
        wo,
        wu,
        wd,
        ffn_normed,
        ffn_hidden,
    )
    for j, scale in enumerate(scales):
        out = (far_out, passing_out)[j % 2]
        out[j // 2] = (joined[j * cells : (j + 1) * cells] * scale[:, :1]).astype(jnp.bfloat16)
    scales, base, chosen = picked((1, 0))
    rest_base[...] = base
    rest_mixed[...] = chosen
    for j, scale in enumerate(scales):
        rest_scale[j * cells : (j + 1) * cells, :] = jnp.broadcast_to(scale, (cells, LANES))


def near_kernel(
    outer,
    tokens,
    anchor_ref,
    anchor_row,
    count_row,
    rest_mixed,
    rest_base,
    rest_scale,
    wo,
    wu,
    wd,
    gain,
    near_out,
    own_out,
    mask_out,
    bound_out,
    ffn_normed,
    ffn_hidden,
):
    slots, cells, width = near_out.shape
    position = lax.axis_index("brick")
    residue = lax.rem(position, WDEP)
    block = lax.div(position, WDEP)
    joined = ffn_rows(
        rest_base[...],
        rest_mixed[...],
        gain[...][None, :],
        wo,
        wu,
        wd,
        ffn_normed,
        ffn_hidden,
    )
    joined = (joined * rest_scale[:, :1]).astype(jnp.bfloat16)
    for s in range(slots):
        near_out[s] = joined[2 * s * cells : (2 * s + 1) * cells]
        own_out[s] = joined[(2 * s + 1) * cells : (2 * s + 2) * cells]
    for rel in range(WDEP):
        for s in range(slots):
            slot = (block * WDEP + (residue ^ rel)) * slots + s
            start = anchor_ref[slot]
            depth = lax.rem(residue + WDEP * NWRAP - start, WDEP)
            step = lax.div(start + depth, WDEP) ^ block
            for k in range(outer):
                row = k * (WDEP * slots) + rel * slots + s
                mask_out[row : row + 1, :] = jnp.full(
                    (1, LANES), jnp.where(step == k, jnp.float32(1), jnp.float32(0)), jnp.float32
                )
    shift = position - anchor_row[...]
    inside = (shift >= 0) & (shift < WDEP)
    centred = shift.astype(jnp.float32) - (WDEP - 1) / 2.0
    spread = WDEP / 4.0
    terms = (
        count_row[...].astype(jnp.float32)
        / (2.0 * tokens)
        * jnp.exp(-centred * centred / (2.0 * spread * spread))
    )
    bound = jnp.maximum(jnp.sum(jnp.where(inside, terms, 0.0), axis=-1, keepdims=True), 1.0)
    bound_out[...] = jnp.broadcast_to(bound, bound_out.shape)


NWRAP = 1 << 20


def in_hbm(array):
    return pltpu.with_memory_space_constraint(array, pltpu.HBM)


def in_vmem(array):
    return pltpu.with_memory_space_constraint(array, pltpu.VMEM)


def limit(mebibytes):
    return pltpu.CompilerParams(vmem_limit_bytes=mebibytes * 1024 * 1024)


def cost(flops, bytes_accessed):
    return pl.CostEstimate(flops=flops, bytes_accessed=bytes_accessed, transcendentals=0)


def far_call(anchor, count, gains, ct_win, pet_win, weights):
    slots, tokens, width = ct_win.shape
    rows = 2 * slots * tokens
    cells = tokens // WDEP
    half = slots * (WDEP // 2) * cells
    rest = pltpu.VMEM((2 * half, width), jnp.bfloat16)
    big = pltpu.VMEM((rows, width), jnp.bfloat16)
    out = pltpu.VMEM((slots, cells, width), jnp.bfloat16)
    passing, far, *passed = pl.pallas_call(
        window_kernel,
        out_shape=[
            out,
            out,
            rest,
            rest,
            pltpu.VMEM((half, LANES), jnp.float32),
        ]
        + [pltpu.VMEM(w.shape, w.dtype) for w in weights[3:]]
        + [pltpu.VMEM((width,), jnp.float32)],
        in_specs=[ANY] * 13,
        out_specs=[VMEM] * 9,
        scratch_shapes=[pltpu.VMEM((width,), jnp.float32)] * 2
        + [pltpu.SMEM(anchor.shape, jnp.int32)] * 2
        + [pltpu.VMEM((2, slots, tokens, width), jnp.bfloat16)]
        + [pltpu.VMEM(w.shape, w.dtype) for w in weights[:3]]
        + [big] * 5
        + [rest, pltpu.VMEM((half, weights[4].shape[1]), jnp.bfloat16)]
        + [pltpu.SemaphoreType.DMA((13,))],
        compiler_params=limit(24),
        name="window_far",
    )(*map(in_hbm, (anchor, count, *gains, ct_win, pet_win, *weights)))
    return passing, far, passed


def near_call(outer, slots, tokens, anchor, count, passed):
    width = passed[0].shape[1]
    cells = tokens // WDEP
    half = slots * (WDEP // 2) * cells
    out = pltpu.VMEM((slots, cells, width), jnp.bfloat16)
    hidden = passed[4].shape[1]
    return pl.pallas_call(
        functools.partial(near_kernel, outer, tokens),
        out_shape=[
            out,
            out,
            pltpu.VMEM((outer * WDEP * slots, LANES), jnp.float32),
            pltpu.VMEM((8, LANES), jnp.float32),
        ],
        in_specs=[SMEM] + [VMEM] * 9,
        out_specs=[VMEM] * 4,
        scratch_shapes=[
            pltpu.VMEM((2 * half, width), jnp.bfloat16),
            pltpu.VMEM((half, hidden), jnp.bfloat16),
        ],
        compiler_params=limit(12),
        cost_estimate=cost(12 * half * width * width, 4 * half * width),
        name="window_near",
    )(in_hbm(anchor), in_hbm(anchor[None, :]), in_hbm(count[None, :]), *map(in_vmem, passed))


def gather_kernel(outer, mask_ref, own, near, far, forward, kept, *sent):
    slots, cells, width = own.shape
    blocks = [own[s] for s in range(slots)] + [near[s] for s in range(slots)]
    blocks += [far[s] for s in range(slots)] + [forward[s] for s in range(slots)]
    blocks = [block.astype(jnp.float32) for block in blocks]
    for k in range(outer):
        total = jnp.zeros((cells, width), jnp.float32)
        for j, block in enumerate(blocks):
            row = k * len(blocks) + j
            mask = jnp.concatenate([mask_ref[row : row + 1, :]] * (width // LANES), axis=1)
            total = total + block * mask
        if k == 0:
            kept[...] = total
        else:
            sent[k - 1][...] = total.astype(jnp.bfloat16)


def gather_call(outer, masks, own, near, far, forward):
    slots, cells, width = own.shape
    return pl.pallas_call(
        functools.partial(gather_kernel, outer),
        out_shape=[pltpu.VMEM((cells, width), jnp.float32)]
        + [pltpu.VMEM((cells, width), jnp.bfloat16)] * (outer - 1),
        in_specs=[VMEM] * 5,
        out_specs=[VMEM] * outer,
        compiler_params=limit(8),
        name="plane_sum",
    )(*map(in_vmem, (masks, own, near, far, forward)))


def upconv_kernel(bound, kept, *refs):
    pieces = refs[:-5]
    weight, up_ref, near_ref, far_ref, grid = refs[-5:]
    channels = up_ref.shape[-1]
    numerator = kept[...]
    for piece in pieces:
        numerator = numerator + piece[...].astype(jnp.float32)
    feature = (numerator / bound[:1, :1]).astype(jnp.bfloat16)
    up_rows = dot(feature, weight[...])
    for a in range(2):
        for b in range(2):
            for c in range(2):
                chunk = (a * 2 + b) * 2 + c
                for y in range(PY):
                    grid[a, 2 * y + b, pl.ds(c, PX, stride=2), :] = up_rows[
                        y * PX : (y + 1) * PX, chunk * channels : (chunk + 1) * channels
                    ]
    upsampled = grid[...].astype(jnp.bfloat16)
    up_ref[...] = upsampled
    even = lax.rem(lax.axis_index("brick"), 2) == 0
    active = jnp.maximum(upsampled, jnp.zeros((), jnp.bfloat16))
    near_ref[...] = jnp.where(even, active[1], active[0])
    far_ref[...] = jnp.where(even, active[0], active[1])


def upconv_call(channels, bound, kept, pieces, weight):
    layer = (2 * PY, 2 * PX, channels)
    return pl.pallas_call(
        upconv_kernel,
        out_shape=[
            pltpu.VMEM((2,) + layer, jnp.bfloat16),
            pltpu.VMEM(layer, jnp.bfloat16),
            pltpu.VMEM(layer, jnp.bfloat16),
        ],
        in_specs=[VMEM] * (3 + len(pieces)),
        out_specs=[VMEM] * 3,
        scratch_shapes=[pltpu.VMEM((2,) + layer, jnp.float32)],
        compiler_params=limit(8),
        name="upconv",
    )(*map(in_vmem, (bound, kept, *pieces, weight)))


def fill_patches(layers, padded, patches):
    height, breadth, channels = layers[0].shape
    rows = height * breadth
    padded[...] = jnp.zeros_like(padded)
    for z, layer in enumerate(layers):
        padded[z, 1 : height + 1, 8 : 8 + breadth, :] = layer.astype(jnp.float32)
    for z in range(len(layers)):
        for dx in range(3):
            column = padded[z, :, 7 + dx : 7 + dx + breadth, :].astype(jnp.bfloat16)
            for dy in range(3):
                tap = dy * 3 + dx
                patches[z * rows : (z + 1) * rows, tap * channels : (tap + 1) * channels] = column[
                    dy : dy + height
                ].reshape(rows, channels)


def conv_local_kernel(up_ref, weight, out_ref, padded, patches):
    depth, height, breadth, channels = up_ref.shape
    rows = height * breadth
    span = 9 * channels
    zero = jnp.zeros((), jnp.bfloat16)
    fill_patches([jnp.maximum(up_ref[z], zero) for z in range(depth)], padded, patches)
    out_ref[...] = up_ref[...].reshape(depth * rows, channels).astype(jnp.float32) + dot(
        patches[...], weight[span : 2 * span, :]
    )
    for z in range(depth - 1):
        out_ref[z * rows : (z + 1) * rows, :] += dot(
            patches[(z + 1) * rows : (z + 2) * rows, :], weight[2 * span :, :]
        )
        out_ref[(z + 1) * rows : (z + 2) * rows, :] += dot(
            patches[z * rows : (z + 1) * rows, :], weight[:span, :]
        )


def conv_halo_kernel(part_ref, near_ref, far_ref, weight, out_ref, padded, patches):
    depth, height, breadth, channels = out_ref.shape
    rows = height * breadth
    span = 9 * channels
    position = lax.axis_index("brick")
    even = lax.rem(position, 2) == 0
    edge = (position == 0) | (position == lax.axis_size("brick") - 1)
    near, far = near_ref[...], far_ref[...]
    far = jnp.where(edge, jnp.zeros_like(far), far)
    fill_patches([jnp.where(even, far, near), jnp.where(even, near, far)], padded, patches)
    for z in range(depth):
        total = part_ref[z * rows : (z + 1) * rows, :]
        if z == 0:
            total = total + dot(patches[:rows, :], weight[:span, :])
        if z == depth - 1:
            total = total + dot(patches[rows:, :], weight[2 * span :, :])
        out_ref[z] = total.astype(jnp.bfloat16).reshape(height, breadth, channels)


def conv_scratch(depth, height, breadth, channels):
    return [
        pltpu.VMEM((depth, height + 2, breadth + 16, channels), jnp.float32),
        pltpu.VMEM((depth * height * breadth, 9 * channels), jnp.bfloat16),
    ]


def conv_local_call(upsampled, weight):
    depth, height, breadth, channels = upsampled.shape
    rows = depth * height * breadth
    return pl.pallas_call(
        conv_local_kernel,
        out_shape=pltpu.VMEM((rows, channels), jnp.float32),
        in_specs=[VMEM] * 2,
        out_specs=VMEM,
        scratch_shapes=conv_scratch(depth, height, breadth, channels),
        compiler_params=limit(8),
        cost_estimate=cost(36 * rows * channels * channels, 12 * rows * channels),
        name="conv_local",
    )(*map(in_vmem, (upsampled, weight)))


def conv_halo_call(shape, part, near, far, weight):
    return pl.pallas_call(
        conv_halo_kernel,
        out_shape=jax.ShapeDtypeStruct(shape, jnp.bfloat16),
        in_specs=[VMEM] * 4,
        out_specs=VMEM,
        scratch_shapes=conv_scratch(2, *shape[1:]),
        compiler_params=limit(8),
        name="conv_halo",
    )(*map(in_vmem, (part, near, far, weight)))


def swap(values, distance, total):
    return lax.ppermute(values, "brick", [(i, i ^ distance) for i in range(total)])


def far_pairs(groups, total):
    pairs = []
    for g in range(groups):
        for i in range(1, total - 1, 2):
            pairs += [(g * total + i, g * total + i + 1), (g * total + i + 1, g * total + i)]
        other = (g ^ 1) if groups % 2 == 0 else g
        pairs += [(g * total + end, other * total + end) for end in (0, total - 1)]
    return pairs


def on_device(
    ct_win,
    pet_win,
    placed_anchor,
    placed_count,
    norm_ct,
    norm_pet,
    norm_ffn,
    w_query,
    w_key,
    w_value,
    w_out,
    w_up,
    w_down,
    w_upconv,
    w_conv,
):
    slots, tokens, _ = ct_win.shape
    channels = w_conv.shape[1]
    total = lax.axis_size("brick")
    outer = total // WDEP
    passing, far, passed = far_call(
        placed_anchor,
        placed_count,
        (norm_ct, norm_pet, norm_ffn),
        ct_win,
        pet_win,
        (w_query, w_key, w_value, w_out, w_up, w_down),
    )
    far = swap(far, 2, total)
    passing = swap(passing, 3, total)
    near, own, masks, bound = near_call(outer, slots, tokens, placed_anchor, placed_count, passed)
    near, far = lax.optimization_barrier((near, far))
    near = swap(near, 1, total)
    kept, *sent = gather_call(outer, masks, own, near, far, passing)
    pieces = [swap(sent[k - 1], k * WDEP, total) for k in range(outer - 1, 0, -1)]
    upsampled, near, far = upconv_call(channels, bound, kept, pieces, w_upconv)
    far = lax.ppermute(far, ("groups", "brick"), far_pairs(lax.axis_size("groups"), total))
    part = conv_local_call(upsampled, w_conv)
    near, part = lax.optimization_barrier((near, part))
    near = swap(near, 1, total)
    return conv_halo_call(upsampled.shape, part, near, far, w_conv)


def solution(mesh):
    return jax.shard_map(
        on_device,
        mesh=mesh,
        in_specs=(
            P(("groups", "brick"), None, None),
            P(("groups", "brick"), None, None),
            P("groups"),
            P("groups"),
            P(),
            P(),
            P(),
            P(),
            P(),
            P(),
            P(),
            P(),
            P(),
            P(),
            P(),
        ),
        out_specs=P(("groups", "brick"), None, None, None),
        check_vma=False,
    )
```

```python
import functools
import math

import jax
import jax.numpy as jnp
from jax import lax
from jax.experimental import pallas as pl
from jax.experimental.pallas import tpu as pltpu
from jax.sharding import PartitionSpec as P

DH = 64
PY = 4
PX = 8
WDEP = 4
LANES = 128

epsilon = 1e-06

VMEM = pl.BlockSpec(memory_space=pltpu.VMEM)
SMEM = pl.BlockSpec(memory_space=pltpu.SMEM)
ANY = pl.BlockSpec(memory_space=pl.ANY)

BELL = [
    math.exp(-((i - (WDEP - 1) / 2.0) ** 2) / (2.0 * (WDEP / 4.0) ** 2)) for i in range(WDEP)
]


def rms_scale(inputs, gain_vec):
    mean_square = jnp.mean(inputs * inputs, axis=-1, keepdims=True)
    return (inputs * lax.rsqrt(mean_square + epsilon) * gain_vec).astype(jnp.bfloat16)


def dot(left, right):
    return jnp.dot(left, right, preferred_element_type=jnp.float32)


def bell_at(depth):
    value = jnp.float32(BELL[0])
    for i in range(1, WDEP):
        value = jnp.where(depth == i, jnp.float32(BELL[i]), value)
    return value


def ffn_rows(base, mixed, gain_row, wo, wu, wd, normed, hidden):
    half = normed.shape[0] // 2
    total = jnp.zeros((half, normed.shape[1]), jnp.float32)
    for m in range(2):
        rows = slice(m * half, (m + 1) * half)
        mid = base[rows].astype(jnp.float32) + dot(mixed[rows], wo[...])
        normed[rows, :] = rms_scale(mid, gain_row)
        total = total + mid
    chunk = hidden.shape[1] // 2
    for c in range(2):
        columns = slice(c * chunk, (c + 1) * chunk)
        both = [
            jax.nn.gelu(dot(normed[m * half : (m + 1) * half, :], wu[:, columns]), approximate=True)
            for m in range(2)
        ]
        hidden[:, columns] = (both[0] + both[1]).astype(jnp.bfloat16)
    return total + dot(hidden[...], wd[...])


def attend(query_ref, key_ref, value_ref, result, place, start, tokens):
    width = query_ref.shape[1]
    low = lax.broadcasted_iota(jnp.int32, (tokens, LANES), 1) < DH
    zero = jnp.zeros((tokens, LANES), jnp.bfloat16)
    one = jnp.ones((tokens, LANES), jnp.bfloat16)
    ones_two = jnp.concatenate([jnp.where(low, one, zero), jnp.where(low, zero, one)], axis=0)
    for pair in range(width // LANES):
        lanes = slice(pair * LANES, (pair + 1) * LANES)
        keys = key_ref[start : start + tokens, lanes]
        values = value_ref[start : start + tokens, lanes]
        keys_two = jnp.concatenate(
            [jnp.where(low, keys, zero), jnp.where(low, zero, keys)], axis=0
        )
        values_two = jnp.concatenate(
            [jnp.where(low, values, zero), jnp.where(low, zero, values)], axis=0
        )
        scores = lax.dot_general(
            query_ref[place : place + tokens, lanes],
            keys_two,
            (((1,), (1,)), ((), ())),
            preferred_element_type=jnp.float32,
        )
        powers = []
        for h in range(2):
            part = scores[:, h * tokens : (h + 1) * tokens]
            top = jnp.max(part, axis=-1, keepdims=True)
            powers.append(jnp.exp((part - top) * (1.0 / DH**0.5)).astype(jnp.bfloat16))
        powers = jnp.concatenate(powers, axis=1)
        both = dot(powers, jnp.concatenate([values_two, ones_two], axis=1))
        result[place : place + tokens, lanes] = (both[:, :LANES] / both[:, LANES:]).astype(
            jnp.bfloat16
        )


def window_kernel(*refs):
    sources, outs, scratch = refs[:13], refs[13:22], refs[22:]
    passing_out, far_out, rest_mixed, rest_base, rest_scale, wo, wu, wd = outs[:8]
    gain_refs = (scratch[0], scratch[1], outs[8])
    anchor_ref, count_ref, tok, wq, wk, wv, normed, q_all, k_all, v_all, mixed = scratch[2:13]
    ffn_normed, ffn_hidden, sems = scratch[13:]
    slots, tokens, width = sources[5].shape
    rows = slots * tokens
    cells = tokens // WDEP
    targets = (
        anchor_ref,
        count_ref,
        *gain_refs,
        tok.at[0],
        tok.at[1],
        wq,
        wk,
        wv,
        wo,
        wu,
        wd,
    )
    copies = [
        pltpu.make_async_copy(src, dst, sems.at[i])
        for i, (src, dst) in enumerate(zip(sources, targets, strict=True))
    ]
    for i in (5, 2, 6, 3, 7, 8, 9, 10, 11, 12, 0, 1, 4):
        copies[i].start()
    position = lax.axis_index("brick")
    residue = lax.rem(position, WDEP)

    copies[2].wait()
    copies[3].wait()
    for m in range(2):
        copies[5 + m].wait()
        for s in range(slots):
            start = m * rows + s * tokens
            normed[start : start + tokens, :] = rms_scale(
                tok[m, s].astype(jnp.float32), gain_refs[m][...][None, :]
            )
    for i, (weight, result) in enumerate(((wq, q_all), (wk, k_all), (wv, v_all))):
        for n in ((7,), (8, 9), ())[i]:
            copies[n].wait()
        for m in range(2):
            half = slice(m * rows, (m + 1) * rows)
            result[half, :] = dot(normed[half, :], weight[...]).astype(jnp.bfloat16)
    for s in range(slots):
        for m in range(2):
            place, start = m * rows + s * tokens, (1 - m) * rows + s * tokens
            attend(q_all, k_all, v_all, mixed, place, start, tokens)
    for i in (0, 1, 4, 10, 11, 12):
        copies[i].wait()

    def picked(rels):
        places, scales = [], []
        for s in range(slots):
            slot = position * slots + s
            factor = jnp.full((1, LANES), count_ref[slot], jnp.int32).astype(jnp.float32) * (
                1.0 / (2.0 * tokens)
            )
            for rel in rels:
                depth = lax.rem((residue ^ rel) + WDEP * NWRAP - anchor_ref[slot], WDEP)
                places.append((s, depth))
                scales.append(factor * bell_at(depth))
        base, chosen = [], []
        for m in range(2):
            for s, depth in places:
                base.append(tok[m, s, pl.ds(pl.multiple_of(depth * cells, cells), cells), :])
                place = pl.multiple_of(m * rows + s * tokens + depth * cells, cells)
                chosen.append(mixed[pl.ds(place, cells), :])
        return scales, jnp.concatenate(base, axis=0), jnp.concatenate(chosen, axis=0)

    scales, base, chosen = picked((2, 3))
    joined = ffn_rows(
        base,
        chosen,
        gain_refs[2][...][None, :],
        wo,
        wu,
        wd,
        ffn_normed,
        ffn_hidden,
    )
    for j, scale in enumerate(scales):
        out = (far_out, passing_out)[j % 2]
        out[j // 2] = (joined[j * cells : (j + 1) * cells] * scale[:, :1]).astype(jnp.bfloat16)
    scales, base, chosen = picked((1, 0))
    rest_base[...] = base
    rest_mixed[...] = chosen
    for j, scale in enumerate(scales):
        rest_scale[j * cells : (j + 1) * cells, :] = jnp.broadcast_to(scale, (cells, LANES))


def near_kernel(
    outer,
    tokens,
    anchor_ref,
    anchor_row,
    count_row,
    rest_mixed,
    rest_base,
    rest_scale,
    wo,
    wu,
    wd,
    gain,
    near_out,
    own_out,
    mask_out,
    bound_out,
    ffn_normed,
    ffn_hidden,
):
    slots, cells, width = near_out.shape
    position = lax.axis_index("brick")
    residue = lax.rem(position, WDEP)
    block = lax.div(position, WDEP)
    joined = ffn_rows(
        rest_base[...],
        rest_mixed[...],
        gain[...][None, :],
        wo,
        wu,
        wd,
        ffn_normed,
        ffn_hidden,
    )
    joined = (joined * rest_scale[:, :1]).astype(jnp.bfloat16)
    for s in range(slots):
        near_out[s] = joined[2 * s * cells : (2 * s + 1) * cells]
        own_out[s] = joined[(2 * s + 1) * cells : (2 * s + 2) * cells]
    for rel in range(WDEP):
        for s in range(slots):
            slot = (block * WDEP + (residue ^ rel)) * slots + s
            start = anchor_ref[slot]
            depth = lax.rem(residue + WDEP * NWRAP - start, WDEP)
            step = lax.div(start + depth, WDEP) ^ block
            for k in range(outer):
                row = k * (WDEP * slots) + rel * slots + s
                mask_out[row : row + 1, :] = jnp.full(
                    (1, LANES), jnp.where(step == k, jnp.float32(1), jnp.float32(0)), jnp.float32
                )
    shift = position - anchor_row[...]
    inside = (shift >= 0) & (shift < WDEP)
    centred = shift.astype(jnp.float32) - (WDEP - 1) / 2.0
    spread = WDEP / 4.0
    terms = (
        count_row[...].astype(jnp.float32)
        / (2.0 * tokens)
        * jnp.exp(-centred * centred / (2.0 * spread * spread))
    )
    bound = jnp.maximum(jnp.sum(jnp.where(inside, terms, 0.0), axis=-1, keepdims=True), 1.0)
    bound_out[...] = jnp.broadcast_to(bound, bound_out.shape)


NWRAP = 1 << 20


def in_hbm(array):
    return pltpu.with_memory_space_constraint(array, pltpu.HBM)


def in_vmem(array):
    return pltpu.with_memory_space_constraint(array, pltpu.VMEM)


def limit(mebibytes):
    return pltpu.CompilerParams(vmem_limit_bytes=mebibytes * 1024 * 1024)


def cost(flops, bytes_accessed):
    return pl.CostEstimate(flops=flops, bytes_accessed=bytes_accessed, transcendentals=0)


def far_call(anchor, count, gains, ct_win, pet_win, weights):
    slots, tokens, width = ct_win.shape
    rows = 2 * slots * tokens
    cells = tokens // WDEP
    half = slots * (WDEP // 2) * cells
    rest = pltpu.VMEM((2 * half, width), jnp.bfloat16)
    big = pltpu.VMEM((rows, width), jnp.bfloat16)
    out = pltpu.VMEM((slots, cells, width), jnp.bfloat16)
    passing, far, *passed = pl.pallas_call(
        window_kernel,
        out_shape=[
            out,
            out,
            rest,
            rest,
            pltpu.VMEM((half, LANES), jnp.float32),
        ]
        + [pltpu.VMEM(w.shape, w.dtype) for w in weights[3:]]
        + [pltpu.VMEM((width,), jnp.float32)],
        in_specs=[ANY] * 13,
        out_specs=[VMEM] * 9,
        scratch_shapes=[pltpu.VMEM((width,), jnp.float32)] * 2
        + [pltpu.SMEM(anchor.shape, jnp.int32)] * 2
        + [pltpu.VMEM((2, slots, tokens, width), jnp.bfloat16)]
        + [pltpu.VMEM(w.shape, w.dtype) for w in weights[:3]]
        + [big] * 5
        + [rest, pltpu.VMEM((half, weights[4].shape[1]), jnp.bfloat16)]
        + [pltpu.SemaphoreType.DMA((13,))],
        compiler_params=limit(24),
        name="window_far",
    )(*map(in_hbm, (anchor, count, *gains, ct_win, pet_win, *weights)))
    return passing, far, passed


def near_call(outer, slots, tokens, anchor, count, passed):
    width = passed[0].shape[1]
    cells = tokens // WDEP
    half = slots * (WDEP // 2) * cells
    out = pltpu.VMEM((slots, cells, width), jnp.bfloat16)
    hidden = passed[4].shape[1]
    return pl.pallas_call(
        functools.partial(near_kernel, outer, tokens),
        out_shape=[
            out,
            out,
            pltpu.VMEM((outer * WDEP * slots, LANES), jnp.float32),
            pltpu.VMEM((8, LANES), jnp.float32),
        ],
        in_specs=[SMEM] + [VMEM] * 9,
        out_specs=[VMEM] * 4,
        scratch_shapes=[
            pltpu.VMEM((2 * half, width), jnp.bfloat16),
            pltpu.VMEM((half, hidden), jnp.bfloat16),
        ],
        compiler_params=limit(12),
        cost_estimate=cost(12 * half * width * width, 4 * half * width),
        name="window_near",
    )(in_hbm(anchor), in_hbm(anchor[None, :]), in_hbm(count[None, :]), *map(in_vmem, passed))


def gather_kernel(outer, mask_ref, own, near, far, forward, kept, *sent):
    slots, cells, width = own.shape
    blocks = [own[s] for s in range(slots)] + [near[s] for s in range(slots)]
    blocks += [far[s] for s in range(slots)] + [forward[s] for s in range(slots)]
    blocks = [block.astype(jnp.float32) for block in blocks]
    for k in range(outer):
        total = jnp.zeros((cells, width), jnp.float32)
        for j, block in enumerate(blocks):
            row = k * len(blocks) + j
            mask = jnp.concatenate([mask_ref[row : row + 1, :]] * (width // LANES), axis=1)
            total = total + block * mask
        if k == 0:
            kept[...] = total
        else:
            sent[k - 1][...] = total.astype(jnp.bfloat16)


def gather_call(outer, masks, own, near, far, forward):
    slots, cells, width = own.shape
    return pl.pallas_call(
        functools.partial(gather_kernel, outer),
        out_shape=[pltpu.VMEM((cells, width), jnp.float32)]
        + [pltpu.VMEM((cells, width), jnp.bfloat16)] * (outer - 1),
        in_specs=[VMEM] * 5,
        out_specs=[VMEM] * outer,
        compiler_params=limit(8),
        name="plane_sum",
    )(*map(in_vmem, (masks, own, near, far, forward)))


def up_layer(feature, weight, start, grid):
    half = weight.shape[1] // 2
    channels = half // 4
    up_rows = dot(feature, weight[:, pl.ds(pl.multiple_of(start * half, half), half)])
    for b in range(2):
        for c in range(2):
            chunk = b * 2 + c
            for y in range(PY):
                grid[2 * y + b, pl.ds(c, PX, stride=2), :] = up_rows[
                    y * PX : (y + 1) * PX, chunk * channels : (chunk + 1) * channels
                ]
    return grid[...].astype(jnp.bfloat16)


def up_far_kernel(bound, kept, *refs):
    pieces = refs[:-4]
    weight, feature_ref, far_ref, grid = refs[-4:]
    numerator = kept[...]
    for piece in pieces:
        numerator = numerator + piece[...].astype(jnp.float32)
    feature = (numerator / bound[:1, :1]).astype(jnp.bfloat16)
    feature_ref[...] = feature
    odd = lax.rem(lax.axis_index("brick"), 2)
    far_ref[...] = up_layer(feature, weight, odd, grid)


def up_far_call(channels, bound, kept, pieces, weight):
    layer = (2 * PY, 2 * PX, channels)
    return pl.pallas_call(
        up_far_kernel,
        out_shape=[pltpu.VMEM(kept.shape, jnp.bfloat16), pltpu.VMEM(layer, jnp.bfloat16)],
        in_specs=[VMEM] * (3 + len(pieces)),
        out_specs=[VMEM] * 2,
        scratch_shapes=[pltpu.VMEM(layer, jnp.float32)],
        compiler_params=limit(8),
        name="up_far",
    )(*map(in_vmem, (bound, kept, *pieces, weight)))


def fill_patches(layers, padded, patches):
    height, breadth, channels = layers[0].shape
    rows = height * breadth
    padded[...] = jnp.zeros_like(padded)
    for z, layer in enumerate(layers):
        padded[z, 1 : height + 1, 8 : 8 + breadth, :] = layer.astype(jnp.float32)
    for z in range(len(layers)):
        for dx in range(3):
            column = padded[z, :, 7 + dx : 7 + dx + breadth, :].astype(jnp.bfloat16)
            for dy in range(3):
                tap = dy * 3 + dx
                patches[z * rows : (z + 1) * rows, tap * channels : (tap + 1) * channels] = column[
                    dy : dy + height
                ].reshape(rows, channels)


def conv_local_kernel(
    feature_ref, far_ref, w_up, weight, near_ref, out_ref, grid, padded, patches
):
    height, breadth, channels = near_ref.shape
    rows = height * breadth
    span = 9 * channels
    even = lax.rem(lax.axis_index("brick"), 2) == 0
    odd = lax.rem(lax.axis_index("brick"), 2)
    near, far = up_layer(feature_ref[...], w_up, 1 - odd, grid), far_ref[...]
    near_ref[...] = near
    layers = [jnp.where(even, far, near), jnp.where(even, near, far)]
    zero = jnp.zeros((), jnp.bfloat16)
    fill_patches([jnp.maximum(layer, zero) for layer in layers], padded, patches)
    both = jnp.concatenate([layer.reshape(rows, channels) for layer in layers], axis=0)
    out_ref[...] = both.astype(jnp.float32) + dot(patches[...], weight[span : 2 * span, :])
    out_ref[:rows, :] += dot(patches[rows:, :], weight[2 * span :, :])
    out_ref[rows:, :] += dot(patches[:rows, :], weight[:span, :])


def conv_halo_kernel(part_ref, near_ref, far_ref, weight, out_ref, padded, patches):
    depth, height, breadth, channels = out_ref.shape
    rows = height * breadth
    span = 9 * channels
    position = lax.axis_index("brick")
    even = lax.rem(position, 2) == 0
    edge = (position == 0) | (position == lax.axis_size("brick") - 1)
    near, far = near_ref[...], far_ref[...]
    near = jnp.maximum(near, jnp.zeros((), jnp.bfloat16))
    far = jnp.where(edge, jnp.zeros_like(far), jnp.maximum(far, jnp.zeros((), jnp.bfloat16)))
    fill_patches([jnp.where(even, far, near), jnp.where(even, near, far)], padded, patches)
    for z in range(depth):
        total = part_ref[z * rows : (z + 1) * rows, :]
        if z == 0:
            total = total + dot(patches[:rows, :], weight[:span, :])
        if z == depth - 1:
            total = total + dot(patches[rows:, :], weight[2 * span :, :])
        out_ref[z] = total.astype(jnp.bfloat16).reshape(height, breadth, channels)


def conv_scratch(depth, height, breadth, channels):
    return [
        pltpu.VMEM((depth, height + 2, breadth + 16, channels), jnp.float32),
        pltpu.VMEM((depth * height * breadth, 9 * channels), jnp.bfloat16),
    ]


def conv_local_call(feature, far, w_up, weight):
    height, breadth, channels = far.shape
    rows = 2 * height * breadth
    return pl.pallas_call(
        conv_local_kernel,
        out_shape=[
            pltpu.VMEM(far.shape, jnp.bfloat16),
            pltpu.VMEM((rows, channels), jnp.float32),
        ],
        in_specs=[VMEM] * 4,
        out_specs=[VMEM] * 2,
        scratch_shapes=[pltpu.VMEM(far.shape, jnp.float32)]
        + conv_scratch(2, height, breadth, channels),
        compiler_params=limit(8),
        cost_estimate=cost(36 * rows * channels * channels, 12 * rows * channels),
        name="conv_local",
    )(*map(in_vmem, (feature, far, w_up, weight)))


def conv_halo_call(shape, part, near, far, weight):
    return pl.pallas_call(
        conv_halo_kernel,
        out_shape=jax.ShapeDtypeStruct(shape, jnp.bfloat16),
        in_specs=[VMEM] * 4,
        out_specs=VMEM,
        scratch_shapes=conv_scratch(2, *shape[1:]),
        compiler_params=limit(8),
        name="conv_halo",
    )(*map(in_vmem, (part, near, far, weight)))


def swap(values, distance, total):
    return lax.ppermute(values, "brick", [(i, i ^ distance) for i in range(total)])


def far_pairs(groups, total):
    pairs = []
    for g in range(groups):
        for i in range(1, total - 1, 2):
            pairs += [(g * total + i, g * total + i + 1), (g * total + i + 1, g * total + i)]
        other = (g ^ 1) if groups % 2 == 0 else g
        pairs += [(g * total + end, other * total + end) for end in (0, total - 1)]
    return pairs


def on_device(
    ct_win,
    pet_win,
    placed_anchor,
    placed_count,
    norm_ct,
    norm_pet,
    norm_ffn,
    w_query,
    w_key,
    w_value,
    w_out,
    w_up,
    w_down,
    w_upconv,
    w_conv,
):
    slots, tokens, _ = ct_win.shape
    channels = w_conv.shape[1]
    total = lax.axis_size("brick")
    outer = total // WDEP
    passing, far, passed = far_call(
        placed_anchor,
        placed_count,
        (norm_ct, norm_pet, norm_ffn),
        ct_win,
        pet_win,
        (w_query, w_key, w_value, w_out, w_up, w_down),
    )
    far = swap(far, 2, total)
    passing = swap(passing, 3, total)
    near, own, masks, bound = near_call(outer, slots, tokens, placed_anchor, placed_count, passed)
    near, far = lax.optimization_barrier((near, far))
    near = swap(near, 1, total)
    kept, *sent = gather_call(outer, masks, own, near, far, passing)
    pieces = [swap(sent[k - 1], k * WDEP, total) for k in range(outer - 1, 0, -1)]
    feature, far = up_far_call(channels, bound, kept, pieces, w_upconv)
    arrived = lax.ppermute(far, ("groups", "brick"), far_pairs(lax.axis_size("groups"), total))
    near, part = conv_local_call(feature, far, w_upconv, w_conv)
    return conv_halo_call((2, *far.shape), part, swap(near, 1, total), arrived, w_conv)


def solution(mesh):
    return jax.shard_map(
        on_device,
        mesh=mesh,
        in_specs=(
            P(("groups", "brick"), None, None),
            P(("groups", "brick"), None, None),
            P("groups"),
            P("groups"),
            P(),
            P(),
            P(),
            P(),
            P(),
            P(),
            P(),
            P(),
            P(),
            P(),
            P(),
        ),
        out_specs=P(("groups", "brick"), None, None, None),
        check_vma=False,
    )
```

```python
import functools
import math

import jax
import jax.numpy as jnp
from jax import lax
from jax.experimental import pallas as pl
from jax.experimental.pallas import tpu as pltpu
from jax.sharding import PartitionSpec as P

DH = 64
PY = 4
PX = 8
WDEP = 4
LANES = 128

epsilon = 1e-06

VMEM = pl.BlockSpec(memory_space=pltpu.VMEM)
SMEM = pl.BlockSpec(memory_space=pltpu.SMEM)
ANY = pl.BlockSpec(memory_space=pl.ANY)

BELL = [
    math.exp(-((i - (WDEP - 1) / 2.0) ** 2) / (2.0 * (WDEP / 4.0) ** 2)) for i in range(WDEP)
]


def rms_scale(inputs, gain_vec):
    mean_square = jnp.mean(inputs * inputs, axis=-1, keepdims=True)
    return (inputs * lax.rsqrt(mean_square + epsilon) * gain_vec).astype(jnp.bfloat16)


def dot(left, right):
    return jnp.dot(left, right, preferred_element_type=jnp.float32)


def bell_at(depth):
    value = jnp.float32(BELL[0])
    for i in range(1, WDEP):
        value = jnp.where(depth == i, jnp.float32(BELL[i]), value)
    return value


def ffn_rows(base, mixed, gain_row, wo, wu, wd, normed, hidden):
    half = normed.shape[0] // 2
    total = jnp.zeros((half, normed.shape[1]), jnp.float32)
    for m in range(2):
        rows = slice(m * half, (m + 1) * half)
        mid = base[rows].astype(jnp.float32) + dot(mixed[rows], wo[...])
        normed[rows, :] = rms_scale(mid, gain_row)
        total = total + mid
    chunk = hidden.shape[1] // 2
    for c in range(2):
        columns = slice(c * chunk, (c + 1) * chunk)
        both = [
            jax.nn.gelu(dot(normed[m * half : (m + 1) * half, :], wu[:, columns]), approximate=True)
            for m in range(2)
        ]
        hidden[:, columns] = (both[0] + both[1]).astype(jnp.bfloat16)
    return total + dot(hidden[...], wd[...])


def attend(query_ref, key_ref, value_ref, result, place, start, tokens):
    width = query_ref.shape[1]
    low = lax.broadcasted_iota(jnp.int32, (tokens, LANES), 1) < DH
    zero = jnp.zeros((tokens, LANES), jnp.bfloat16)
    one = jnp.ones((tokens, LANES), jnp.bfloat16)
    ones_two = jnp.concatenate([jnp.where(low, one, zero), jnp.where(low, zero, one)], axis=0)
    for pair in range(width // LANES):
        lanes = slice(pair * LANES, (pair + 1) * LANES)
        keys = key_ref[start : start + tokens, lanes]
        values = value_ref[start : start + tokens, lanes]
        keys_two = jnp.concatenate(
            [jnp.where(low, keys, zero), jnp.where(low, zero, keys)], axis=0
        )
        values_two = jnp.concatenate(
            [jnp.where(low, values, zero), jnp.where(low, zero, values)], axis=0
        )
        scores = lax.dot_general(
            query_ref[place : place + tokens, lanes],
            keys_two,
            (((1,), (1,)), ((), ())),
            preferred_element_type=jnp.float32,
        )
        powers = []
        for h in range(2):
            part = scores[:, h * tokens : (h + 1) * tokens]
            top = jnp.max(part, axis=-1, keepdims=True)
            powers.append(jnp.exp((part - top) * (1.0 / DH**0.5)).astype(jnp.bfloat16))
        powers = jnp.concatenate(powers, axis=1)
        both = dot(powers, jnp.concatenate([values_two, ones_two], axis=1))
        result[place : place + tokens, lanes] = (both[:, :LANES] / both[:, LANES:]).astype(
            jnp.bfloat16
        )


def picked(rels, anchor_ref, count_ref, tok, mixed):
    slots, tokens = tok.shape[1:3]
    rows = slots * tokens
    cells = tokens // WDEP
    position = lax.axis_index("brick")
    residue = lax.rem(position, WDEP)
    places, scales = [], []
    for s in range(slots):
        slot = position * slots + s
        factor = jnp.full((1, LANES), count_ref[slot], jnp.int32).astype(jnp.float32) * (
            1.0 / (2.0 * tokens)
        )
        for rel in rels:
            depth = lax.rem((residue ^ rel) + WDEP * NWRAP - anchor_ref[slot], WDEP)
            places.append((s, depth))
            scales.append(factor * bell_at(depth))
    base, chosen = [], []
    for m in range(2):
        for s, depth in places:
            base.append(tok[m, s, pl.ds(pl.multiple_of(depth * cells, cells), cells), :])
            place = pl.multiple_of(m * rows + s * tokens + depth * cells, cells)
            chosen.append(mixed[pl.ds(place, cells), :])
    return scales, jnp.concatenate(base, axis=0), jnp.concatenate(chosen, axis=0)


def window_kernel(*refs):
    sources, outs, scratch = refs[:13], refs[13:21], refs[21:]
    passing_out, far_out, mixed, tok, wo, wu, wd = outs[:7]
    gain_refs = (scratch[0], scratch[1], outs[7])
    anchor_ref, count_ref, wq, wk, wv, normed, q_all, k_all, v_all = scratch[2:11]
    ffn_normed, ffn_hidden, sems = scratch[11:]
    slots, tokens, width = sources[5].shape
    rows = slots * tokens
    cells = tokens // WDEP
    targets = (
        anchor_ref,
        count_ref,
        *gain_refs,
        tok.at[0],
        tok.at[1],
        wq,
        wk,
        wv,
        wo,
        wu,
        wd,
    )
    copies = [
        pltpu.make_async_copy(src, dst, sems.at[i])
        for i, (src, dst) in enumerate(zip(sources, targets, strict=True))
    ]
    for i in (5, 2, 6, 3, 7, 8, 9, 10, 11, 12, 0, 1, 4):
        copies[i].start()

    copies[2].wait()
    copies[3].wait()
    for m in range(2):
        copies[5 + m].wait()
        for s in range(slots):
            start = m * rows + s * tokens
            normed[start : start + tokens, :] = rms_scale(
                tok[m, s].astype(jnp.float32), gain_refs[m][...][None, :]
            )
    for i, (weight, result) in enumerate(((wq, q_all), (wk, k_all), (wv, v_all))):
        for n in ((7,), (8, 9), ())[i]:
            copies[n].wait()
        for m in range(2):
            half = slice(m * rows, (m + 1) * rows)
            result[half, :] = dot(normed[half, :], weight[...]).astype(jnp.bfloat16)
    for s in range(slots):
        for m in range(2):
            place, start = m * rows + s * tokens, (1 - m) * rows + s * tokens
            attend(q_all, k_all, v_all, mixed, place, start, tokens)
    for i in (0, 1, 4, 10, 11, 12):
        copies[i].wait()

    scales, base, chosen = picked((2, 3), anchor_ref, count_ref, tok, mixed)
    joined = ffn_rows(
        base,
        chosen,
        gain_refs[2][...][None, :],
        wo,
        wu,
        wd,
        ffn_normed,
        ffn_hidden,
    )
    for j, scale in enumerate(scales):
        out = (far_out, passing_out)[j % 2]
        out[j // 2] = (joined[j * cells : (j + 1) * cells] * scale[:, :1]).astype(jnp.bfloat16)


def near_kernel(
    outer,
    tokens,
    anchor_ref,
    count_ref,
    anchor_row,
    count_row,
    all_mixed,
    tok,
    wo,
    wu,
    wd,
    gain,
    near_out,
    own_out,
    mask_out,
    bound_out,
    ffn_normed,
    ffn_hidden,
):
    slots, cells, width = near_out.shape
    position = lax.axis_index("brick")
    residue = lax.rem(position, WDEP)
    block = lax.div(position, WDEP)
    scales, base, chosen = picked((1, 0), anchor_ref, count_ref, tok, all_mixed)
    joined = ffn_rows(
        base,
        chosen,
        gain[...][None, :],
        wo,
        wu,
        wd,
        ffn_normed,
        ffn_hidden,
    )
    for j, scale in enumerate(scales):
        out = (near_out, own_out)[j % 2]
        out[j // 2] = (joined[j * cells : (j + 1) * cells] * scale[:, :1]).astype(jnp.bfloat16)
    for rel in range(WDEP):
        for s in range(slots):
            slot = (block * WDEP + (residue ^ rel)) * slots + s
            start = anchor_ref[slot]
            depth = lax.rem(residue + WDEP * NWRAP - start, WDEP)
            step = lax.div(start + depth, WDEP) ^ block
            for k in range(outer):
                row = k * (WDEP * slots) + rel * slots + s
                mask_out[row : row + 1, :] = jnp.full(
                    (1, LANES), jnp.where(step == k, jnp.float32(1), jnp.float32(0)), jnp.float32
                )
    shift = position - anchor_row[...]
    inside = (shift >= 0) & (shift < WDEP)
    centred = shift.astype(jnp.float32) - (WDEP - 1) / 2.0
    spread = WDEP / 4.0
    terms = (
        count_row[...].astype(jnp.float32)
        / (2.0 * tokens)
        * jnp.exp(-centred * centred / (2.0 * spread * spread))
    )
    bound = jnp.maximum(jnp.sum(jnp.where(inside, terms, 0.0), axis=-1, keepdims=True), 1.0)
    bound_out[...] = jnp.broadcast_to(bound, bound_out.shape)


NWRAP = 1 << 20


def in_hbm(array):
    return pltpu.with_memory_space_constraint(array, pltpu.HBM)


def in_vmem(array):
    return pltpu.with_memory_space_constraint(array, pltpu.VMEM)


def limit(mebibytes):
    return pltpu.CompilerParams(vmem_limit_bytes=mebibytes * 1024 * 1024)


def cost(flops, bytes_accessed):
    return pl.CostEstimate(flops=flops, bytes_accessed=bytes_accessed, transcendentals=0)


def far_call(anchor, count, gains, ct_win, pet_win, weights):
    slots, tokens, width = ct_win.shape
    rows = 2 * slots * tokens
    cells = tokens // WDEP
    half = slots * (WDEP // 2) * cells
    rest = pltpu.VMEM((2 * half, width), jnp.bfloat16)
    big = pltpu.VMEM((rows, width), jnp.bfloat16)
    out = pltpu.VMEM((slots, cells, width), jnp.bfloat16)
    passing, far, *passed = pl.pallas_call(
        window_kernel,
        out_shape=[
            out,
            out,
            big,
            pltpu.VMEM((2, slots, tokens, width), jnp.bfloat16),
        ]
        + [pltpu.VMEM(w.shape, w.dtype) for w in weights[3:]]
        + [pltpu.VMEM((width,), jnp.float32)],
        in_specs=[ANY] * 13,
        out_specs=[VMEM] * 8,
        scratch_shapes=[pltpu.VMEM((width,), jnp.float32)] * 2
        + [pltpu.SMEM(anchor.shape, jnp.int32)] * 2
        + [pltpu.VMEM(w.shape, w.dtype) for w in weights[:3]]
        + [big] * 4
        + [rest, pltpu.VMEM((half, weights[4].shape[1]), jnp.bfloat16)]
        + [pltpu.SemaphoreType.DMA((13,))],
        compiler_params=limit(24),
        name="window_far",
    )(*map(in_hbm, (anchor, count, *gains, ct_win, pet_win, *weights)))
    return passing, far, passed


def near_call(outer, slots, tokens, anchor, count, passed):
    width = passed[0].shape[1]
    cells = tokens // WDEP
    half = slots * (WDEP // 2) * cells
    out = pltpu.VMEM((slots, cells, width), jnp.bfloat16)
    hidden = passed[3].shape[1]
    return pl.pallas_call(
        functools.partial(near_kernel, outer, tokens),
        out_shape=[
            out,
            out,
            pltpu.VMEM((outer * WDEP * slots, LANES), jnp.float32),
            pltpu.VMEM((8, LANES), jnp.float32),
        ],
        in_specs=[SMEM] * 2 + [VMEM] * 8,
        out_specs=[VMEM] * 4,
        scratch_shapes=[
            pltpu.VMEM((2 * half, width), jnp.bfloat16),
            pltpu.VMEM((half, hidden), jnp.bfloat16),
        ],
        compiler_params=limit(12),
        cost_estimate=cost(12 * half * width * width, 4 * half * width),
        name="window_near",
    )(
        in_hbm(anchor),
        in_hbm(count),
        in_hbm(anchor[None, :]),
        in_hbm(count[None, :]),
        *map(in_vmem, passed),
    )


def gather_kernel(outer, mask_ref, own, near, far, forward, kept, *sent):
    slots, cells, width = own.shape
    blocks = [own[s] for s in range(slots)] + [near[s] for s in range(slots)]
    blocks += [far[s] for s in range(slots)] + [forward[s] for s in range(slots)]
    blocks = [block.astype(jnp.float32) for block in blocks]
    for k in range(outer):
        total = jnp.zeros((cells, width), jnp.float32)
        for j, block in enumerate(blocks):
            row = k * len(blocks) + j
            mask = jnp.concatenate([mask_ref[row : row + 1, :]] * (width // LANES), axis=1)
            total = total + block * mask
        if k == 0:
            kept[...] = total
        else:
            sent[k - 1][...] = total.astype(jnp.bfloat16)


def gather_call(outer, masks, own, near, far, forward):
    slots, cells, width = own.shape
    return pl.pallas_call(
        functools.partial(gather_kernel, outer),
        out_shape=[pltpu.VMEM((cells, width), jnp.float32)]
        + [pltpu.VMEM((cells, width), jnp.bfloat16)] * (outer - 1),
        in_specs=[VMEM] * 5,
        out_specs=[VMEM] * outer,
        compiler_params=limit(8),
        name="plane_sum",
    )(*map(in_vmem, (masks, own, near, far, forward)))


def up_layer(feature, weight, start, grid):
    half = weight.shape[1] // 2
    channels = half // 4
    up_rows = dot(feature, weight[:, pl.ds(pl.multiple_of(start * half, half), half)])
    for b in range(2):
        for c in range(2):
            chunk = b * 2 + c
            for y in range(PY):
                grid[2 * y + b, pl.ds(c, PX, stride=2), :] = up_rows[
                    y * PX : (y + 1) * PX, chunk * channels : (chunk + 1) * channels
                ]
    return grid[...].astype(jnp.bfloat16)


def up_far_kernel(bound, kept, *refs):
    pieces = refs[:-4]
    weight, feature_ref, far_ref, grid = refs[-4:]
    numerator = kept[...]
    for piece in pieces:
        numerator = numerator + piece[...].astype(jnp.float32)
    feature = (numerator / bound[:1, :1]).astype(jnp.bfloat16)
    feature_ref[...] = feature
    odd = lax.rem(lax.axis_index("brick"), 2)
    far_ref[...] = up_layer(feature, weight, odd, grid)


def up_far_call(channels, bound, kept, pieces, weight):
    layer = (2 * PY, 2 * PX, channels)
    return pl.pallas_call(
        up_far_kernel,
        out_shape=[pltpu.VMEM(kept.shape, jnp.bfloat16), pltpu.VMEM(layer, jnp.bfloat16)],
        in_specs=[VMEM] * (3 + len(pieces)),
        out_specs=[VMEM] * 2,
        scratch_shapes=[pltpu.VMEM(layer, jnp.float32)],
        compiler_params=limit(8),
        name="up_far",
    )(*map(in_vmem, (bound, kept, *pieces, weight)))


def fill_patches(layers, padded, patches):
    height, breadth, channels = layers[0].shape
    rows = height * breadth
    padded[...] = jnp.zeros_like(padded)
    for z, layer in enumerate(layers):
        padded[z, 1 : height + 1, 8 : 8 + breadth, :] = layer.astype(jnp.float32)
    for z in range(len(layers)):
        for dx in range(3):
            column = padded[z, :, 7 + dx : 7 + dx + breadth, :].astype(jnp.bfloat16)
            for dy in range(3):
                tap = dy * 3 + dx
                patches[z * rows : (z + 1) * rows, tap * channels : (tap + 1) * channels] = column[
                    dy : dy + height
                ].reshape(rows, channels)


def conv_local_kernel(
    feature_ref, far_ref, w_up, weight, near_ref, out_ref, grid, padded, patches
):
    height, breadth, channels = near_ref.shape
    rows = height * breadth
    span = 9 * channels
    even = lax.rem(lax.axis_index("brick"), 2) == 0
    odd = lax.rem(lax.axis_index("brick"), 2)
    near, far = up_layer(feature_ref[...], w_up, 1 - odd, grid), far_ref[...]
    near_ref[...] = near
    layers = [jnp.where(even, far, near), jnp.where(even, near, far)]
    zero = jnp.zeros((), jnp.bfloat16)
    fill_patches([jnp.maximum(layer, zero) for layer in layers], padded, patches)
    both = jnp.concatenate([layer.reshape(rows, channels) for layer in layers], axis=0)
    out_ref[...] = both.astype(jnp.float32) + dot(patches[...], weight[span : 2 * span, :])
    out_ref[:rows, :] += dot(patches[rows:, :], weight[2 * span :, :])
    out_ref[rows:, :] += dot(patches[:rows, :], weight[:span, :])


def conv_halo_kernel(part_ref, near_ref, far_ref, weight, out_ref, padded, patches):
    depth, height, breadth, channels = out_ref.shape
    rows = height * breadth
    span = 9 * channels
    position = lax.axis_index("brick")
    even = lax.rem(position, 2) == 0
    edge = (position == 0) | (position == lax.axis_size("brick") - 1)
    near, far = near_ref[...], far_ref[...]
    near = jnp.maximum(near, jnp.zeros((), jnp.bfloat16))
    far = jnp.where(edge, jnp.zeros_like(far), jnp.maximum(far, jnp.zeros((), jnp.bfloat16)))
    fill_patches([jnp.where(even, far, near), jnp.where(even, near, far)], padded, patches)
    for z in range(depth):
        total = part_ref[z * rows : (z + 1) * rows, :]
        if z == 0:
            total = total + dot(patches[:rows, :], weight[:span, :])
        if z == depth - 1:
            total = total + dot(patches[rows:, :], weight[2 * span :, :])
        out_ref[z] = total.astype(jnp.bfloat16).reshape(height, breadth, channels)


def conv_scratch(depth, height, breadth, channels):
    return [
        pltpu.VMEM((depth, height + 2, breadth + 16, channels), jnp.float32),
        pltpu.VMEM((depth * height * breadth, 9 * channels), jnp.bfloat16),
    ]


def conv_local_call(feature, far, w_up, weight):
    height, breadth, channels = far.shape
    rows = 2 * height * breadth
    return pl.pallas_call(
        conv_local_kernel,
        out_shape=[
            pltpu.VMEM(far.shape, jnp.bfloat16),
            pltpu.VMEM((rows, channels), jnp.float32),
        ],
        in_specs=[VMEM] * 4,
        out_specs=[VMEM] * 2,
        scratch_shapes=[pltpu.VMEM(far.shape, jnp.float32)]
        + conv_scratch(2, height, breadth, channels),
        compiler_params=limit(8),
        cost_estimate=cost(36 * rows * channels * channels, 12 * rows * channels),
        name="conv_local",
    )(*map(in_vmem, (feature, far, w_up, weight)))


def conv_halo_call(shape, part, near, far, weight):
    return pl.pallas_call(
        conv_halo_kernel,
        out_shape=jax.ShapeDtypeStruct(shape, jnp.bfloat16),
        in_specs=[VMEM] * 4,
        out_specs=VMEM,
        scratch_shapes=conv_scratch(2, *shape[1:]),
        compiler_params=limit(8),
        name="conv_halo",
    )(*map(in_vmem, (part, near, far, weight)))


def swap(values, distance, total):
    return lax.ppermute(values, "brick", [(i, i ^ distance) for i in range(total)])


def far_pairs(groups, total):
    pairs = []
    for g in range(groups):
        for i in range(1, total - 1, 2):
            pairs += [(g * total + i, g * total + i + 1), (g * total + i + 1, g * total + i)]
        other = (g ^ 1) if groups % 2 == 0 else g
        pairs += [(g * total + end, other * total + end) for end in (0, total - 1)]
    return pairs


def on_device(
    ct_win,
    pet_win,
    placed_anchor,
    placed_count,
    norm_ct,
    norm_pet,
    norm_ffn,
    w_query,
    w_key,
    w_value,
    w_out,
    w_up,
    w_down,
    w_upconv,
    w_conv,
):
    slots, tokens, _ = ct_win.shape
    channels = w_conv.shape[1]
    total = lax.axis_size("brick")
    outer = total // WDEP
    passing, far, passed = far_call(
        placed_anchor,
        placed_count,
        (norm_ct, norm_pet, norm_ffn),
        ct_win,
        pet_win,
        (w_query, w_key, w_value, w_out, w_up, w_down),
    )
    far = swap(far, 2, total)
    passing = swap(passing, 3, total)
    near, own, masks, bound = near_call(outer, slots, tokens, placed_anchor, placed_count, passed)
    near, far = lax.optimization_barrier((near, far))
    near = swap(near, 1, total)
    kept, *sent = gather_call(outer, masks, own, near, far, passing)
    pieces = [swap(sent[k - 1], k * WDEP, total) for k in sorted(range(1, outer), key=lambda k: (abs(2 * k - outer), -k))]
    feature, far = up_far_call(channels, bound, kept, pieces, w_upconv)
    arrived = lax.ppermute(far, ("groups", "brick"), far_pairs(lax.axis_size("groups"), total))
    near, part = conv_local_call(feature, far, w_upconv, w_conv)
    return conv_halo_call((2, *far.shape), part, swap(near, 1, total), arrived, w_conv)


def solution(mesh):
    return jax.shard_map(
        on_device,
        mesh=mesh,
        in_specs=(
            P(("groups", "brick"), None, None),
            P(("groups", "brick"), None, None),
            P("groups"),
            P("groups"),
            P(),
            P(),
            P(),
            P(),
            P(),
            P(),
            P(),
            P(),
            P(),
            P(),
            P(),
        ),
        out_specs=P(("groups", "brick"), None, None, None),
        check_vma=False,
    )
```
